128 devices in a mesh: lon: 8 (over y, core), lat: 16 (over x, z).
Axes of the slice: x: 4, y: 4, z: 4, core: 2. Of those that a mesh axis runs over, the one named last changes fastest.
Arguments:
- grid: bfloat16 [12, 2, 2, 1024, 4096], P(None, None, None, 'lat', 'lon'), may hold values from -6 to 6
- legendre: bfloat16 [8, 128, 1024, 2, 512], P('lon', None, 'lat'), may hold values from -0.25 to 0.25
Outputs:
- spectral: float32 [8, 128, 8, 2, 2, 2, 512], P('lon', 'lat')
The draws below stay inside these ranges and needn't reach their ends.
All inputs are finite; a program needn't handle non-finite values.
Results may differ from the reference program's by a relative error of at most 0.0029.
Values sent between devices are 32-bit elements; how exact they have to be, the bound alone decides.
A program may use at most 128 MiB of HBM per device.

```python
import math
import jax
import jax.numpy as jnp
import numpy as np
from jax import lax

NLON = 4096
WAVES = 1024
FIELDS = 12
LEV = 2
NHALF = 1024
WAVE_DEV = 128
N_LON = 8


def spiked(values, own_key, source, target, shards_of, factor):
    owner, partner = [(jnp.arange(values.shape[dim]) // (values.shape[dim] // shards_of)).reshape([-1 if axis == dim else 1 for axis in range(values.ndim)]) for dim in (source, target)]
    chosen = jax.random.permutation(own_key, shards_of)[partner]
    strong = (owner == chosen) | (owner == (partner + shards_of // 2) % shards_of)
    return jnp.where(strong, factor * values, values)


def levels(key, shape, split, smallest, largest):
    def one(dim, blocks):
        draws = jax.random.uniform(jax.random.fold_in(jax.random.fold_in(key, 6), dim), (blocks,), jnp.float32, smallest / len(split), largest / len(split))
        return jnp.repeat(jnp.exp(draws), shape[dim] // blocks).reshape((-1,) + (1,) * (len(shape) - dim - 1))

    gain = one(*split[0])
    for cut in split[1:]:
        gain = gain * one(*cut)
    return gain


def gaussian(rng, dims, scale, limit, shards=(), kind=jnp.bfloat16):
    entries = jax.random.normal(rng, dims, jnp.float32) * scale
    if len(shards) > 0:
        entries = levels(rng, dims, shards, -0.22, 0.18) * entries
    return jnp.clip(entries, min=-limit, max=limit).astype(kind)


def heavy_noise(stream_key, extent, width, reach, shards, heavy, held_as=jnp.bfloat16):
    values = width * jax.random.normal(stream_key, extent, jnp.float32)
    if shards:
        values = values * levels(stream_key, extent, shards, -0.22, 0.18)
    return jnp.clip(spiked(values, jax.random.fold_in(stream_key, 3), *heavy), -reach, reach).astype(held_as)


def setup_inputs(seed: int = 0) -> dict:
    key_list = jax.random.split(jax.random.key(seed), 3)
    return {
        "grid": gaussian(key_list[0], (FIELDS, LEV, 2, NHALF, NLON), 1.0, 6.0, ((3, 16), (4, 8))),
        "legendre": heavy_noise(key_list[1], (N_LON, WAVE_DEV, NHALF, 2, WAVES // 2), NHALF ** -0.5, 0.25, ((0, 8), (2, 16)), (2, 1, 16, 2.0)),
    }


adiabatic_exponent = 0.286

def tendency_fields(numeric_buffer_grid):
    eastward_flow_speed, poleward_flow_speed, local_spin_field, flow_spreading_rate = (numeric_buffer_grid[0], numeric_buffer_grid[1], numeric_buffer_grid[2], numeric_buffer_grid[3])
    kinetic_warmth_field, water_vapour_mixing = (numeric_buffer_grid[4], numeric_buffer_grid[5])
    warmth_eastward_slope, warmth_poleward_slope = (numeric_buffer_grid[6], numeric_buffer_grid[7])
    vapour_eastward_slope, vapour_poleward_slope = (numeric_buffer_grid[8], numeric_buffer_grid[9])
    ground_load_eastward_slope, ground_load_poleward_slope = (numeric_buffer_grid[10], numeric_buffer_grid[11])
    return jnp.stack([local_spin_field * poleward_flow_speed - kinetic_warmth_field * ground_load_eastward_slope, -local_spin_field * eastward_flow_speed - kinetic_warmth_field * ground_load_poleward_slope, eastward_flow_speed * poleward_flow_speed, -(eastward_flow_speed * warmth_eastward_slope + poleward_flow_speed * warmth_poleward_slope) + adiabatic_exponent * kinetic_warmth_field * flow_spreading_rate, -(eastward_flow_speed * vapour_eastward_slope + poleward_flow_speed * vapour_poleward_slope) - water_vapour_mixing * flow_spreading_rate, eastward_flow_speed * kinetic_warmth_field, poleward_flow_speed * kinetic_warmth_field, poleward_flow_speed * water_vapour_mixing], 0)

def reference(grid, legendre):
    devices = N_LON
    per_device = WAVES // devices
    order = np.arange(WAVES).reshape(per_device, devices).T

    def level_spectra(level_grid):
        tendencies = tendency_fields(level_grid.astype(jnp.float32))
        spectrum = jnp.fft.rfft(tendencies, axis=-1)[..., :WAVES] / math.sqrt(NLON)
        parts = jnp.stack([jnp.real(spectrum), jnp.imag(spectrum)], 3)
        return parts[..., order]
    spectra = lax.map(level_spectra, jnp.moveaxis(grid, 1, 0))
    northern = spectra[:, :, 0]
    southern = spectra[:, :, 1]
    folded = jnp.stack([northern + southern, northern - southern], 0).astype(jnp.bfloat16)
    moved = jnp.moveaxis(folded, 5, 0)

    def project(pair):
        section, weights = pair
        return jnp.einsum('elkjcs,sjeh->sklceh', section.astype(jnp.float32), weights.astype(jnp.float32))
    result = lax.map(project, (moved, legendre))
    wavenumber = jnp.asarray(order, dtype=jnp.int32)[:, :, None, None]
    degree = 2 * jnp.arange(WAVES // 2, dtype=jnp.int32)[None, None, None, :] + jnp.arange(2, dtype=jnp.int32)[None, None, :, None]
    inside = wavenumber + degree < WAVES
    return jnp.where(inside[:, :, None, None, None], result, jnp.zeros((), jnp.float32))
```

```python
import jax
import jax.numpy as jnp
import numpy as np
from jax import lax
from jax.experimental import pallas as pl
from jax.experimental.pallas import tpu as pltpu
from jax.sharding import PartitionSpec as P

NLON = 4096
WAVES = 1024
LON_DEV = 8
LAT_DEV = 16
LON_LOCAL = NLON // LON_DEV
ROWS = 2048
CHUNKS = 8
UNITS = (4, 3, 2, 1)
OFFSETS = (0, 4, 7, 9)
TOTAL = 10
ADIABATIC = 0.286
ROOT_HALF = 0.5**0.5


def phase_table():
    i, core, y, k = np.meshgrid(
        np.arange(CHUNKS), np.arange(2), np.arange(4), np.arange(LAT_DEV), indexing="ij"
    )
    m = 2 * y + core + LON_DEV * (CHUNKS * k + i)
    turns = m[..., None] * np.arange(LON_LOCAL) % NLON
    angles = turns * (2.0 * np.pi / NLON)
    table = np.stack([np.cos(angles), -np.sin(angles)], 3) / np.sqrt(NLON)
    return table.reshape(CHUNKS, 8, 2, LAT_DEV, LON_LOCAL).astype(np.float32)


def eighth_cos(n):
    n = lax.rem(n, 8)
    value = jnp.float32(1.0)
    for at, root in ((1, ROOT_HALF), (2, 0.0), (3, -ROOT_HALF), (4, -1.0), (5, -ROOT_HALF), (6, 0.0), (7, ROOT_HALF)):
        value = jnp.where(n == at, jnp.float32(root), value)
    return value


def tendencies(f):
    u, v, zeta, div, temp, hum, temp_x, temp_y, hum_x, hum_y, press_x, press_y = f
    return (
        zeta * v - temp * press_x,
        -zeta * u - temp * press_y,
        u * v,
        -(u * temp_x + v * temp_y) + ADIABATIC * temp * div,
        -(u * hum_x + v * hum_y) - hum * div,
        u * temp,
        v * temp,
        v * hum,
    )


def split_bf16(a):
    high = a.astype(jnp.bfloat16)
    return high, (a - high.astype(jnp.float32)).astype(jnp.bfloat16)


NT = (((1,), (1,)), ((), ()))


def kernel(
    grid_ref, table_ref, leg_ref, out_ref,
    t_hi, t_lo, mix, table, phases, part, paired, y1_in, y2_in, fold, leg, spec, z1_in, z2_in, x_in,
    table_sem, leg_sem, core_s, core_r, y1_s, y1_r, y2_s, y2_r, z1_s, z1_r, z2_s, z2_r, x_s, x_r,
):
    r = lax.axis_index("lon")
    k = lax.axis_index("lat")
    y, core = r // 2, lax.rem(r, 2)
    x, z = k // 4, lax.rem(k, 4)
    y_up, y_down = lax.rem(y + 1, 4), lax.rem(y + 3, 4)
    z_up, z_down = lax.rem(z + 1, 4), lax.rem(z + 3, 4)
    y_far, z_far = lax.rem(y + 2, 4), lax.rem(z + 2, 4)

    def lon_dev(yy, cc):
        return {"lon": yy * 2 + cc}

    def lat_dev(xx, zz):
        return {"lat": xx * 4 + zz}

    def send(src, dst, s, q, dev):
        return pltpu.make_async_remote_copy(
            src_ref=src, dst_ref=dst, send_sem=s, recv_sem=q, device_id=dev, device_id_type=pl.DeviceIdType.MESH
        )

    def table_copy(t):
        return pltpu.make_async_copy(table_ref.at[t], table.at[t], table_sem.at[t])

    def leg_copy(t):
        slot = lax.rem(t, 2)
        return pltpu.make_async_copy(leg_ref.at[:, t], leg.at[slot], leg_sem.at[slot])

    def core_copy(t):
        return send(
            part.at[lax.rem(t, 2), 1 - core], paired.at[t], core_s.at[t], core_r.at[t], lon_dev(y, 1 - core)
        )

    def y1_copies(t):
        return (
            send(paired.at[t, y_far, 0], y1_in.at[t, 0], y1_s.at[t, 0], y1_r.at[t, 0], lon_dev(y_up, core)),
            send(paired.at[t, y_far, 1], y1_in.at[t, 1], y1_s.at[t, 1], y1_r.at[t, 1], lon_dev(y_down, core)),
        )

    def y2_copies(t):
        return (
            send(paired.at[t, y_up], y2_in.at[t, 0], y2_s.at[t, 0], y2_r.at[t, 0], lon_dev(y_up, core)),
            send(paired.at[t, y_down], y2_in.at[t, 1], y2_s.at[t, 1], y2_r.at[t, 1], lon_dev(y_down, core)),
        )

    half = TOTAL // 2

    def z1_copies(t):
        return (
            send(spec.at[t, z_far, 0:half], z1_in.at[t, 0], z1_s.at[t, 0], z1_r.at[t, 0], lat_dev(x, z_up)),
            send(spec.at[t, z_far, half:TOTAL], z1_in.at[t, 1], z1_s.at[t, 1], z1_r.at[t, 1], lat_dev(x, z_down)),
        )

    def z2_copies(t):
        return (
            send(spec.at[t, z_up], z2_in.at[t, 0], z2_s.at[t, 0], z2_r.at[t, 0], lat_dev(x, z_up)),
            send(spec.at[t, z_down], z2_in.at[t, 1], z2_s.at[t, 1], z2_r.at[t, 1], lat_dev(x, z_down)),
        )

    def x_copy(t, source, to):
        n, first = UNITS[to], OFFSETS[to]
        return send(
            spec.at[t, z, first : first + n], x_in.at[t, source, 0:n], x_s.at[t, to], x_r.at[t, source], lat_dev(to, z)
        )

    for t in range(CHUNKS):
        table_copy(t).start()
    for t in range(2):
        leg_copy(t).start()

    barrier = pltpu.get_barrier_semaphore()
    for dev in (lon_dev(y, 1 - core), lon_dev(y_up, core), lon_dev(y_down, core), lat_dev(x, z_up), lat_dev(x, z_down)):
        pl.semaphore_signal(barrier, inc=1, device_id=dev, device_id_type=pl.DeviceIdType.MESH)
    for step in range(1, 4):
        dev = lat_dev(lax.rem(x + step, 4), z)
        pl.semaphore_signal(barrier, inc=1, device_id=dev, device_id_type=pl.DeviceIdType.MESH)

    def fields(step, carry):
        level, block = step // 4, lax.rem(step, 4)
        first = pl.multiple_of(block * 16, 16)
        for lane in range(4):
            lanes = pl.ds(lane * 128, 128)
            north, south = (
                tendencies([grid_ref[f, level, h, pl.ds(first, 16), lanes].astype(jnp.float32) for f in range(12)])
                for h in range(2)
            )
            for t in range(8):
                mix[lane * 8 + t, pl.ds(0, 16, stride=2), :] = north[t] + south[t]
                mix[lane * 8 + t, pl.ds(1, 16, stride=2), :] = north[t] - south[t]
            for t in range(8):
                high, low = split_bf16(mix[lane * 8 + t])
                at = pl.multiple_of((2 * t + level) * 128 + block * 32, 32)
                t_hi[pl.ds(at, 32), lanes] = high
                t_lo[pl.ds(at, 32), lanes] = low
        return carry

    lax.fori_loop(0, 8, fields, 0)

    pl.semaphore_wait(barrier, 8)

    def analyse(t):
        slot = lax.rem(t, 2)
        table_copy(t).wait()

        def rotate(block, carry):
            q = 2 * lax.rem(block, 4) + block // 4
            c, s = eighth_cos(r * q), eighth_cos(r * q + 6)
            real, imag = table[t, block, 0], table[t, block, 1]
            for part_index, value in enumerate((real * c + imag * s, imag * c - real * s)):
                high, low = split_bf16(value)
                at = pl.multiple_of(block * 32 + part_index * 16, 16)
                phases[pl.ds(at, 16), :] = high
                phases[pl.ds(at + 256, 16), :] = low
            return carry

        lax.fori_loop(0, 8, rotate, 0)

        @pl.when(t >= 2)
        def _():
            core_copy(t - 2).wait_send()

        def columns(n, carry):
            rows = pl.ds(pl.multiple_of(n * 256, 256), 256)
            both = lax.dot_general(phases[...], t_hi[rows, :], NT, preferred_element_type=jnp.float32)
            rest = lax.dot_general(phases[0:256, :], t_lo[rows, :], NT, preferred_element_type=jnp.float32)
            value = both[0:256] + (both[256:512] + rest)
            part[slot, :, :, :, :, rows] = value.reshape(2, 4, 2, 16, 256)
            return carry

        lax.fori_loop(0, 8, columns, 0)
        core_copy(t).start()

    def pair_sum(t):
        slot = lax.rem(t, 2)
        core_copy(t).wait_recv()

        def add(n, carry):
            yy = lax.rem(y_far + n, 4)
            paired[t, yy] = paired[t, yy] + part[slot, core, yy]
            return carry

        lax.fori_loop(0, 4, add, 0)
        for copy in y1_copies(t):
            copy.start()

    def y_forward(t):
        for copy in y1_copies(t):
            copy.wait_recv()
        paired[t, y_up, 0] = paired[t, y_up, 0] + y1_in[t, 0]
        paired[t, y_down, 1] = paired[t, y_down, 1] + y1_in[t, 1]
        for copy in y2_copies(t):
            copy.start()

    def project(t):
        slot = lax.rem(t, 2)
        for copy in y2_copies(t):
            copy.wait_recv()
        for c in range(2):
            for tl in range(16):
                lanes = pl.ds(tl * 128, 128)
                value = paired[t, y, c, :, lanes] + (y2_in[t, 0, c, :, lanes] + y2_in[t, 1, c, :, lanes])
                fold[pl.ds(tl * 2 + c, 16, stride=32), :] = value
        leg_copy(t).wait()
        even = lax.rem(lax.broadcasted_iota(jnp.int32, (32, 128), 1), 2) == 0
        for owner in range(LAT_DEV):
            ox, oz = owner // 4, owner % 4
            rows = fold[owner * 32 : owner * 32 + 32, :]
            zero = jnp.zeros_like(rows)
            left = jnp.concatenate([jnp.where(even, rows, zero), jnp.where(even, zero, rows)], 0).astype(jnp.bfloat16)
            n = UNITS[ox]
            right = leg[slot, owner, :, :, 0 : 128 * n].reshape(128, 128 * n)
            value = jnp.dot(left, right, preferred_element_type=jnp.float32)
            for unit in range(n):
                spec[t, oz, OFFSETS[ox] + unit] = value[:, unit * 128 : unit * 128 + 128]
        for copy in z1_copies(t):
            copy.start()

        @pl.when(t + 2 < CHUNKS)
        def _():
            leg_copy(t + 2).start()

    def z_forward(t):
        for copy in z1_copies(t):
            copy.wait_recv()
        spec[t, z_up, 0:half] = spec[t, z_up, 0:half] + z1_in[t, 0]
        spec[t, z_down, half:TOTAL] = spec[t, z_down, half:TOTAL] + z1_in[t, 1]
        for copy in z2_copies(t):
            copy.start()

    def x_start(t):
        for copy in z2_copies(t):
            copy.wait_recv()
        spec[t, z] = spec[t, z] + (z2_in[t, 0] + z2_in[t, 1])
        for to in range(4):

            @pl.when(x != to)
            def _():
                x_copy(t, x, to).start()

    def finish(t):
        order = r + LON_DEV * (CHUNKS * k + t)
        for mine in range(4):

            @pl.when(x == mine)
            def _():
                n, first = UNITS[mine], OFFSETS[mine]
                others = [source for source in range(4) if source != mine]
                for source in others:
                    x_copy(t, source, mine).wait_recv()
                lane = lax.broadcasted_iota(jnp.int32, (32, 128), 1)
                for unit in range(4):
                    for e in range(2):
                        lanes = pl.ds(e * 512 + unit * 128, 128)
                        if unit >= n:
                            out_ref[t, :, lanes] = jnp.zeros((32, 128), jnp.float32)
                            continue
                        rows = pl.ds(e * 32, 32)
                        value = spec[t, z, first + unit, rows, :]
                        for source in others:
                            value = value + x_in[t, source, unit, rows, :]
                        inside = order + 2 * (lane + unit * 128) + e < WAVES
                        out_ref[t, :, lanes] = jnp.where(inside, value, jnp.zeros_like(value))

    def stage(run, t):
        @pl.when((t >= 0) & (t < CHUNKS))
        def _():
            run(t)

    def steps(step, carry):
        t = step - 2
        stage(y_forward, t)
        stage(project, t - 1)
        stage(x_start, t - 2)
        stage(analyse, t + 2)
        stage(z_forward, t - 1)
        stage(pair_sum, t + 2)
        stage(finish, t - 3)
        return carry

    lax.fori_loop(0, CHUNKS + 5, steps, 0)

    def drain(t, carry):
        @pl.when(t >= CHUNKS - 2)
        def _():
            core_copy(t).wait_send()

        for copy in (*y1_copies(t), *y2_copies(t), *z1_copies(t), *z2_copies(t)):
            copy.wait_send()
        for to in range(4):

            @pl.when(x != to)
            def _():
                x_copy(t, x, to).wait_send()

        return carry

    lax.fori_loop(0, CHUNKS, drain, 0)


def local(grid, legendre):
    table = jnp.asarray(phase_table())
    f32, bf16 = jnp.float32, jnp.bfloat16
    dma = pltpu.SemaphoreType.DMA
    result = pl.pallas_call(
        kernel,
        out_shape=jax.ShapeDtypeStruct((CHUNKS, 32, WAVES), f32),
        in_specs=[
            pl.BlockSpec(memory_space=pltpu.VMEM),
            pl.BlockSpec(memory_space=pl.ANY),
            pl.BlockSpec(memory_space=pl.ANY),
        ],
        out_specs=pl.BlockSpec(memory_space=pltpu.VMEM),
        scratch_shapes=[
            pltpu.VMEM((ROWS, LON_LOCAL), bf16),
            pltpu.VMEM((ROWS, LON_LOCAL), bf16),
            pltpu.VMEM((32, 32, 128), f32),
            pltpu.VMEM((CHUNKS, 8, 2, 16, LON_LOCAL), f32),
            pltpu.VMEM((512, LON_LOCAL), bf16),
            pltpu.VMEM((2, 2, 4, 2, 16, ROWS), f32),
            pltpu.VMEM((CHUNKS, 4, 2, 16, ROWS), f32),
            pltpu.VMEM((CHUNKS, 2, 16, ROWS), f32),
            pltpu.VMEM((CHUNKS, 2, 2, 16, ROWS), f32),
            pltpu.VMEM((512, 128), f32),
            pltpu.VMEM((2, 16, 64, 2, 512), bf16),
            pltpu.VMEM((CHUNKS, 4, TOTAL, 64, 128), f32),
            pltpu.VMEM((CHUNKS, 2, TOTAL // 2, 64, 128), f32),
            pltpu.VMEM((CHUNKS, 2, TOTAL, 64, 128), f32),
            pltpu.VMEM((CHUNKS, 4, 4, 64, 128), f32),
            dma((CHUNKS,)),
            dma((2,)),
            dma((CHUNKS,)),
            dma((CHUNKS,)),
            *[dma((CHUNKS, 2)) for _ in range(8)],
            dma((CHUNKS, 4)),
            dma((CHUNKS, 4)),
        ],
        compiler_params=pltpu.CompilerParams(
            collective_id=0, has_side_effects=True, vmem_limit_bytes=62 * 2**20
        ),
        name="spectral",
    )(grid, table, legendre.reshape(LAT_DEV, CHUNKS, 64, 2, 512))
    return result.reshape(1, CHUNKS, 8, 2, 2, 2, 512)


def solution(mesh):
    in_specs = (P(None, None, None, "lat", "lon"), P("lon", None, "lat", None, None))
    out_specs = P("lon", "lat", None, None, None, None, None)
    return jax.shard_map(local, mesh=mesh, in_specs=in_specs, out_specs=out_specs, check_vma=False)
```

```python
import jax
import jax.numpy as jnp
import numpy as np
from jax import lax
from jax.experimental import pallas as pl
from jax.experimental.pallas import tpu as pltpu
from jax.sharding import PartitionSpec as P

NLON = 4096
WAVES = 1024
LON_DEV = 8
LAT_DEV = 16
LON_LOCAL = NLON // LON_DEV
ROWS = 2048
CHUNKS = 8
UNITS = (4, 3, 2, 1)
Z_UNITS = (3, 2, 1, 0)
Z_OFFSETS = (0, 3, 5, 6)
Z_TOTAL = 6
ADIABATIC = 0.286
ROOT_HALF = 0.5**0.5


def phase_table():
    i, core, y, k = np.meshgrid(
        np.arange(CHUNKS), np.arange(2), np.arange(4), np.arange(LAT_DEV), indexing="ij"
    )
    m = 2 * y + core + LON_DEV * (CHUNKS * k + i)
    turns = m[..., None] * np.arange(LON_LOCAL) % NLON
    angles = turns * (2.0 * np.pi / NLON)
    table = np.stack([np.cos(angles), -np.sin(angles)], 3) / np.sqrt(NLON)
    return table.reshape(CHUNKS, 8, 2, LAT_DEV, LON_LOCAL).astype(np.float32)


def eighth_cos(n):
    n = lax.rem(n, 8)
    value = jnp.float32(1.0)
    for at, root in ((1, ROOT_HALF), (2, 0.0), (3, -ROOT_HALF), (4, -1.0), (5, -ROOT_HALF), (6, 0.0), (7, ROOT_HALF)):
        value = jnp.where(n == at, jnp.float32(root), value)
    return value


def tendencies(f):
    u, v, zeta, div, temp, hum, temp_x, temp_y, hum_x, hum_y, press_x, press_y = f
    return (
        zeta * v - temp * press_x,
        -zeta * u - temp * press_y,
        u * v,
        -(u * temp_x + v * temp_y) + ADIABATIC * temp * div,
        -(u * hum_x + v * hum_y) - hum * div,
        u * temp,
        v * temp,
        v * hum,
    )


def split_bf16(a):
    high = a.astype(jnp.bfloat16)
    return high, (a - high.astype(jnp.float32)).astype(jnp.bfloat16)


NT = (((1,), (1,)), ((), ()))


def kernel(
    grid_ref, table_ref, leg_ref, out_ref,
    t_hi, t_lo, mix, table, phases, part, paired, y1_in, y2_in, fold, leg,
    spec_z, spec_x, z1_in, z2_in, zx_in, x1_in, x2_in, xz_in,
    table_sem, leg_sem, core_s, core_r, y1_s, y1_r, y2_s, y2_r,
    z1_s, z1_r, z2_s, z2_r, x1_s, x1_r, x2_s, x2_r, zx_s, zx_r, xz_s, xz_r,
):
    r = lax.axis_index("lon")
    k = lax.axis_index("lat")
    y, core = r // 2, lax.rem(r, 2)
    x, z = k // 4, lax.rem(k, 4)
    y_up, y_down = lax.rem(y + 1, 4), lax.rem(y + 3, 4)
    z_up, z_down = lax.rem(z + 1, 4), lax.rem(z + 3, 4)
    x_up, x_down = lax.rem(x + 1, 4), lax.rem(x + 3, 4)
    x_far, y_far, z_far = lax.rem(x + 2, 4), lax.rem(y + 2, 4), lax.rem(z + 2, 4)

    def lon_dev(yy, cc):
        return {"lon": yy * 2 + cc}

    def lat_dev(xx, zz):
        return {"lat": xx * 4 + zz}

    def send(src, dst, s, q, dev):
        return pltpu.make_async_remote_copy(
            src_ref=src, dst_ref=dst, send_sem=s, recv_sem=q, device_id=dev, device_id_type=pl.DeviceIdType.MESH
        )

    def table_copy(t):
        return pltpu.make_async_copy(table_ref.at[t], table.at[t], table_sem.at[t])

    def leg_copy(t):
        slot = lax.rem(t, 2)
        return pltpu.make_async_copy(leg_ref.at[:, t], leg.at[slot], leg_sem.at[slot])

    def core_copy(t):
        return send(
            part.at[lax.rem(t, 2), 1 - core], paired.at[t], core_s.at[t], core_r.at[t], lon_dev(y, 1 - core)
        )

    def y1_copies(t):
        return (
            send(paired.at[t, y_far, 0], y1_in.at[t, 0], y1_s.at[t, 0], y1_r.at[t, 0], lon_dev(y_up, core)),
            send(paired.at[t, y_far, 1], y1_in.at[t, 1], y1_s.at[t, 1], y1_r.at[t, 1], lon_dev(y_down, core)),
        )

    def y2_copies(t):
        return (
            send(paired.at[t, y_up], y2_in.at[t, 0], y2_s.at[t, 0], y2_r.at[t, 0], lon_dev(y_up, core)),
            send(paired.at[t, y_down], y2_in.at[t, 1], y2_s.at[t, 1], y2_r.at[t, 1], lon_dev(y_down, core)),
        )

    z_half = Z_TOTAL // 2

    def z1_copies(t):
        return (
            send(spec_z.at[t, z_far, 0:z_half], z1_in.at[t, 0], z1_s.at[t, 0], z1_r.at[t, 0], lat_dev(x, z_up)),
            send(spec_z.at[t, z_far, z_half:Z_TOTAL], z1_in.at[t, 1], z1_s.at[t, 1], z1_r.at[t, 1], lat_dev(x, z_down)),
        )

    def z2_copies(t):
        return (
            send(spec_z.at[t, z_up], z2_in.at[t, 0], z2_s.at[t, 0], z2_r.at[t, 0], lat_dev(x, z_up)),
            send(spec_z.at[t, z_down], z2_in.at[t, 1], z2_s.at[t, 1], z2_r.at[t, 1], lat_dev(x, z_down)),
        )

    def x1_copies(t):
        return (
            send(spec_x.at[t, x_far, 0:2], x1_in.at[t, 0], x1_s.at[t, 0], x1_r.at[t, 0], lat_dev(x_up, z)),
            send(spec_x.at[t, x_far, 2:4], x1_in.at[t, 1], x1_s.at[t, 1], x1_r.at[t, 1], lat_dev(x_down, z)),
        )

    def x2_copies(t):
        return (
            send(spec_x.at[t, x_up], x2_in.at[t, 0], x2_s.at[t, 0], x2_r.at[t, 0], lat_dev(x_up, z)),
            send(spec_x.at[t, x_down], x2_in.at[t, 1], x2_s.at[t, 1], x2_r.at[t, 1], lat_dev(x_down, z)),
        )

    def zx_copy(t, source, to):
        n, first = Z_UNITS[to], Z_OFFSETS[to]
        return send(
            spec_z.at[t, z, first : first + n], zx_in.at[t, source, 0:n], zx_s.at[t, to], zx_r.at[t, source], lat_dev(to, z)
        )

    def xz_copies(t):
        copies = []
        for step in range(1, 4):
            to = lax.rem(z + step, 4)
            copies.append(
                send(spec_x.at[t, x, to], xz_in.at[t, step - 1], xz_s.at[t, step - 1], xz_r.at[t, step - 1], lat_dev(x, to))
            )
        return copies

    for t in range(CHUNKS):
        table_copy(t).start()
    for t in range(2):
        leg_copy(t).start()

    barrier = pltpu.get_barrier_semaphore()
    neighbours = [lon_dev(y, 1 - core), lon_dev(y_up, core), lon_dev(y_down, core)]
    neighbours += [lat_dev(x, to) for to in (z_up, z_far, z_down)] + [lat_dev(to, z) for to in (x_up, x_far, x_down)]
    for dev in neighbours:
        pl.semaphore_signal(barrier, inc=1, device_id=dev, device_id_type=pl.DeviceIdType.MESH)

    def fields(step, carry):
        level, block = step // 4, lax.rem(step, 4)
        first = pl.multiple_of(block * 16, 16)
        for lane in range(4):
            lanes = pl.ds(lane * 128, 128)
            north, south = (
                tendencies([grid_ref[f, level, h, pl.ds(first, 16), lanes].astype(jnp.float32) for f in range(12)])
                for h in range(2)
            )
            for t in range(8):
                mix[lane * 8 + t, pl.ds(0, 16, stride=2), :] = north[t] + south[t]
                mix[lane * 8 + t, pl.ds(1, 16, stride=2), :] = north[t] - south[t]
            for t in range(8):
                high, low = split_bf16(mix[lane * 8 + t])
                at = pl.multiple_of((2 * t + level) * 128 + block * 32, 32)
                t_hi[pl.ds(at, 32), lanes] = high
                t_lo[pl.ds(at, 32), lanes] = low
        return carry

    lax.fori_loop(0, 8, fields, 0)

    pl.semaphore_wait(barrier, len(neighbours))

    def analyse(t):
        slot = lax.rem(t, 2)
        table_copy(t).wait()

        def rotate(block, carry):
            q = 2 * lax.rem(block, 4) + block // 4
            c, s = eighth_cos(r * q), eighth_cos(r * q + 6)
            real, imag = table[t, block, 0], table[t, block, 1]
            for part_index, value in enumerate((real * c + imag * s, imag * c - real * s)):
                high, low = split_bf16(value)
                at = pl.multiple_of(block * 32 + part_index * 16, 16)
                phases[pl.ds(at, 16), :] = high
                phases[pl.ds(at + 256, 16), :] = low
            return carry

        lax.fori_loop(0, 8, rotate, 0)

        @pl.when(t >= 2)
        def _():
            core_copy(t - 2).wait_send()

        def columns(n, carry):
            rows = pl.ds(pl.multiple_of(n * 256, 256), 256)
            both = lax.dot_general(phases[...], t_hi[rows, :], NT, preferred_element_type=jnp.float32)
            rest = lax.dot_general(phases[0:256, :], t_lo[rows, :], NT, preferred_element_type=jnp.float32)
            value = both[0:256] + (both[256:512] + rest)
            part[slot, :, :, :, :, rows] = value.reshape(2, 4, 2, 16, 256)
            return carry

        lax.fori_loop(0, 8, columns, 0)
        core_copy(t).start()

    def pair_sum(t):
        slot = lax.rem(t, 2)
        core_copy(t).wait_recv()

        def add(n, carry):
            yy = lax.rem(y_far + n, 4)
            paired[t, yy] = paired[t, yy] + part[slot, core, yy]
            return carry

        lax.fori_loop(0, 4, add, 0)
        for copy in y1_copies(t):
            copy.start()

    def y_forward(t):
        for copy in y1_copies(t):
            copy.wait_recv()
        paired[t, y_up, 0] = paired[t, y_up, 0] + y1_in[t, 0]
        paired[t, y_down, 1] = paired[t, y_down, 1] + y1_in[t, 1]
        for copy in y2_copies(t):
            copy.start()

    def project(t):
        slot = lax.rem(t, 2)
        for copy in y2_copies(t):
            copy.wait_recv()
        for c in range(2):
            for tl in range(16):
                lanes = pl.ds(tl * 128, 128)
                value = paired[t, y, c, :, lanes] + (y2_in[t, 0, c, :, lanes] + y2_in[t, 1, c, :, lanes])
                fold[pl.ds(tl * 2 + c, 16, stride=32), :] = value
        leg_copy(t).wait()
        even = lax.rem(lax.broadcasted_iota(jnp.int32, (32, 128), 1), 2) == 0
        for owner in range(LAT_DEV):
            ox, oz = owner // 4, owner % 4
            rows = fold[owner * 32 : owner * 32 + 32, :]
            zero = jnp.zeros_like(rows)
            left = jnp.concatenate([jnp.where(even, rows, zero), jnp.where(even, zero, rows)], 0).astype(jnp.bfloat16)
            n = UNITS[ox]
            right = leg[slot, owner, :, :, 0 : 128 * n].reshape(128, 128 * n)
            value = jnp.dot(left, right, preferred_element_type=jnp.float32)
            for unit in range(n - 1):
                spec_z[t, oz, Z_OFFSETS[ox] + unit] = value[:, unit * 128 : unit * 128 + 128]
            spec_x[t, ox, oz] = value[:, (n - 1) * 128 : n * 128]
        for copy in (*z1_copies(t), *x1_copies(t)):
            copy.start()

        @pl.when(t + 2 < CHUNKS)
        def _():
            leg_copy(t + 2).start()

    def forward(t):
        for copy in z1_copies(t):
            copy.wait_recv()
        spec_z[t, z_up, 0:z_half] = spec_z[t, z_up, 0:z_half] + z1_in[t, 0]
        spec_z[t, z_down, z_half:Z_TOTAL] = spec_z[t, z_down, z_half:Z_TOTAL] + z1_in[t, 1]
        for copy in z2_copies(t):
            copy.start()
        for copy in x1_copies(t):
            copy.wait_recv()
        spec_x[t, x_up, 0:2] = spec_x[t, x_up, 0:2] + x1_in[t, 0]
        spec_x[t, x_down, 2:4] = spec_x[t, x_down, 2:4] + x1_in[t, 1]
        for copy in x2_copies(t):
            copy.start()

    def cross(t):
        for copy in z2_copies(t):
            copy.wait_recv()
        spec_z[t, z] = spec_z[t, z] + (z2_in[t, 0] + z2_in[t, 1])
        for to in range(3):

            @pl.when(x != to)
            def _():
                zx_copy(t, x, to).start()

        for copy in x2_copies(t):
            copy.wait_recv()
        spec_x[t, x] = spec_x[t, x] + (x2_in[t, 0] + x2_in[t, 1])
        for copy in xz_copies(t):
            copy.start()

    def finish(t):
        order = r + LON_DEV * (CHUNKS * k + t)
        lane = lax.broadcasted_iota(jnp.int32, (32, 128), 1)
        for copy in xz_copies(t):
            copy.wait_recv()

        def write(unit, e, value):
            inside = order + 2 * (lane + unit * 128) + e < WAVES
            out_ref[t, :, pl.ds(e * 512 + unit * 128, 128)] = jnp.where(inside, value, jnp.zeros_like(value))

        for mine in range(4):

            @pl.when(x == mine)
            def _():
                n, first = Z_UNITS[mine], Z_OFFSETS[mine]
                others = [source for source in range(4) if source != mine]
                for source in others if n else ():
                    zx_copy(t, source, mine).wait_recv()
                for e in range(2):
                    rows = pl.ds(e * 32, 32)
                    for unit in range(n):
                        value = spec_z[t, z, first + unit, rows, :]
                        for source in others:
                            value = value + zx_in[t, source, unit, rows, :]
                        write(unit, e, value)
                    value = spec_x[t, mine, z, rows, :]
                    for step in range(3):
                        value = value + xz_in[t, step, rows, :]
                    write(n, e, value)
                    for unit in range(n + 1, 4):
                        out_ref[t, :, pl.ds(e * 512 + unit * 128, 128)] = jnp.zeros((32, 128), jnp.float32)

    def stage(run, t):
        @pl.when((t >= 0) & (t < CHUNKS))
        def _():
            run(t)

    def steps(step, carry):
        t = step - 2
        stage(y_forward, t)
        stage(project, t - 1)
        stage(cross, t - 2)
        stage(analyse, t + 2)
        stage(forward, t - 1)
        stage(pair_sum, t + 2)
        stage(finish, t - 3)
        return carry

    lax.fori_loop(0, CHUNKS + 5, steps, 0)

    def drain(t, carry):
        @pl.when(t >= CHUNKS - 2)
        def _():
            core_copy(t).wait_send()

        ring = (*y1_copies(t), *y2_copies(t), *z1_copies(t), *z2_copies(t), *x1_copies(t), *x2_copies(t))
        for copy in (*ring, *xz_copies(t)):
            copy.wait_send()
        for to in range(3):

            @pl.when(x != to)
            def _():
                zx_copy(t, x, to).wait_send()

        return carry

    lax.fori_loop(0, CHUNKS, drain, 0)


def local(grid, legendre):
    table = jnp.asarray(phase_table())
    f32, bf16 = jnp.float32, jnp.bfloat16
    dma = pltpu.SemaphoreType.DMA
    result = pl.pallas_call(
        kernel,
        out_shape=jax.ShapeDtypeStruct((CHUNKS, 32, WAVES), f32),
        in_specs=[
            pl.BlockSpec(memory_space=pltpu.VMEM),
            pl.BlockSpec(memory_space=pl.ANY),
            pl.BlockSpec(memory_space=pl.ANY),
        ],
        out_specs=pl.BlockSpec(memory_space=pltpu.VMEM),
        scratch_shapes=[
            pltpu.VMEM((ROWS, LON_LOCAL), bf16),
            pltpu.VMEM((ROWS, LON_LOCAL), bf16),
            pltpu.VMEM((32, 32, 128), f32),
            pltpu.VMEM((CHUNKS, 8, 2, 16, LON_LOCAL), f32),
            pltpu.VMEM((512, LON_LOCAL), bf16),
            pltpu.VMEM((2, 2, 4, 2, 16, ROWS), f32),
            pltpu.VMEM((CHUNKS, 4, 2, 16, ROWS), f32),
            pltpu.VMEM((CHUNKS, 2, 16, ROWS), f32),
            pltpu.VMEM((CHUNKS, 2, 2, 16, ROWS), f32),
            pltpu.VMEM((512, 128), f32),
            pltpu.VMEM((2, 16, 64, 2, 512), bf16),
            pltpu.VMEM((CHUNKS, 4, Z_TOTAL, 64, 128), f32),
            pltpu.VMEM((CHUNKS, 4, 4, 64, 128), f32),
            pltpu.VMEM((CHUNKS, 2, Z_TOTAL // 2, 64, 128), f32),
            pltpu.VMEM((CHUNKS, 2, Z_TOTAL, 64, 128), f32),
            pltpu.VMEM((CHUNKS, 4, 3, 64, 128), f32),
            pltpu.VMEM((CHUNKS, 2, 2, 64, 128), f32),
            pltpu.VMEM((CHUNKS, 2, 4, 64, 128), f32),
            pltpu.VMEM((CHUNKS, 3, 64, 128), f32),
            dma((CHUNKS,)),
            dma((2,)),
            dma((CHUNKS,)),
            dma((CHUNKS,)),
            *[dma((CHUNKS, 2)) for _ in range(12)],
            *[dma((CHUNKS, 4)) for _ in range(2)],
            *[dma((CHUNKS, 3)) for _ in range(2)],
        ],
        compiler_params=pltpu.CompilerParams(
            collective_id=0, has_side_effects=True, vmem_limit_bytes=62 * 2**20
        ),
        name="spectral",
    )(grid, table, legendre.reshape(LAT_DEV, CHUNKS, 64, 2, 512))
    return result.reshape(1, CHUNKS, 8, 2, 2, 2, 512)


def solution(mesh):
    in_specs = (P(None, None, None, "lat", "lon"), P("lon", None, "lat", None, None))
    out_specs = P("lon", "lat", None, None, None, None, None)
    return jax.shard_map(local, mesh=mesh, in_specs=in_specs, out_specs=out_specs, check_vma=False)
```

```python
import jax
import jax.numpy as jnp
import numpy as np
from jax import lax
from jax.experimental import pallas as pl
from jax.experimental.pallas import tpu as pltpu
from jax.sharding import PartitionSpec as P

NLON = 4096
WAVES = 1024
LON_DEV = 8
LAT_DEV = 16
LON_LOCAL = NLON // LON_DEV
ROWS = 1024
CHUNKS = 8
LEVELS = 2
STEPS = CHUNKS * LEVELS
UNITS = (4, 3, 2, 1)
Z_UNITS = (3, 2, 1, 0)
Z_OFFSETS = (0, 3, 5, 6)
Z_TOTAL = 6
ADIABATIC = 0.286
ROOT_HALF = 0.5**0.5


def phase_table():
    i, core, y, k = np.meshgrid(
        np.arange(CHUNKS), np.arange(2), np.arange(4), np.arange(LAT_DEV), indexing="ij"
    )
    m = 2 * y + core + LON_DEV * (CHUNKS * k + i)
    turns = m[..., None] * np.arange(LON_LOCAL) % NLON
    angles = turns * (2.0 * np.pi / NLON)
    table = np.stack([np.cos(angles), -np.sin(angles)], 3) / np.sqrt(NLON)
    return table.reshape(CHUNKS, 8, 2, LAT_DEV, LON_LOCAL).astype(np.float32)


def eighth_cos(n):
    n = lax.rem(n, 8)
    value = jnp.float32(1.0)
    for at, root in ((1, ROOT_HALF), (2, 0.0), (3, -ROOT_HALF), (4, -1.0), (5, -ROOT_HALF), (6, 0.0), (7, ROOT_HALF)):
        value = jnp.where(n == at, jnp.float32(root), value)
    return value


def tendencies(f):
    u, v, zeta, div, temp, hum, temp_x, temp_y, hum_x, hum_y, press_x, press_y = f
    return (
        zeta * v - temp * press_x,
        -zeta * u - temp * press_y,
        u * v,
        -(u * temp_x + v * temp_y) + ADIABATIC * temp * div,
        -(u * hum_x + v * hum_y) - hum * div,
        u * temp,
        v * temp,
        v * hum,
    )


def split_bf16(a):
    high = a.astype(jnp.bfloat16)
    return high, (a - high.astype(jnp.float32)).astype(jnp.bfloat16)


NT = (((1,), (1,)), ((), ()))


def kernel(
    grid_ref, table_ref, leg_ref, out_ref,
    grid, t_hi, t_lo, mix, table, phases, part, paired, y1_in, y2_in, fold, leg,
    spec_z, spec_x, z1_in, z2_in, zx_in, x1_in, x2_in, xz_in,
    grid_sem, table_sem, leg_sem, core_s, core_r, y1_s, y1_r, y2_s, y2_r,
    z1_s, z1_r, z2_s, z2_r, x1_s, x1_r, x2_s, x2_r, zx_s, zx_r, xz_s, xz_r,
):
    r = lax.axis_index("lon")
    k = lax.axis_index("lat")
    y, core = r // 2, lax.rem(r, 2)
    x, z = k // 4, lax.rem(k, 4)
    y_up, y_down = lax.rem(y + 1, 4), lax.rem(y + 3, 4)
    z_up, z_down = lax.rem(z + 1, 4), lax.rem(z + 3, 4)
    x_up, x_down = lax.rem(x + 1, 4), lax.rem(x + 3, 4)
    x_far, y_far, z_far = lax.rem(x + 2, 4), lax.rem(y + 2, 4), lax.rem(z + 2, 4)

    def lon_dev(yy, cc):
        return {"lon": yy * 2 + cc}

    def lat_dev(xx, zz):
        return {"lat": xx * 4 + zz}

    def send(src, dst, s, q, dev):
        return pltpu.make_async_remote_copy(
            src_ref=src, dst_ref=dst, send_sem=s, recv_sem=q, device_id=dev, device_id_type=pl.DeviceIdType.MESH
        )

    def table_copy(t):
        return pltpu.make_async_copy(table_ref.at[t], table.at[t], table_sem.at[t])

    def leg_copy(i):
        slot = lax.rem(i, 2)
        return pltpu.make_async_copy(leg_ref.at[:, i], leg.at[slot], leg_sem.at[slot])

    def grid_copy(level):
        return pltpu.make_async_copy(grid_ref.at[:, level], grid.at[level], grid_sem.at[level])

    def core_copy(t):
        return send(
            part.at[lax.rem(t, 2), 1 - core], paired.at[t], core_s.at[t], core_r.at[t], lon_dev(y, 1 - core)
        )

    def y1_copies(t):
        return (
            send(paired.at[t, y_far, 0], y1_in.at[t, 0], y1_s.at[t, 0], y1_r.at[t, 0], lon_dev(y_up, core)),
            send(paired.at[t, y_far, 1], y1_in.at[t, 1], y1_s.at[t, 1], y1_r.at[t, 1], lon_dev(y_down, core)),
        )

    def y2_copies(t):
        return (
            send(paired.at[t, y_up], y2_in.at[t, 0], y2_s.at[t, 0], y2_r.at[t, 0], lon_dev(y_up, core)),
            send(paired.at[t, y_down], y2_in.at[t, 1], y2_s.at[t, 1], y2_r.at[t, 1], lon_dev(y_down, core)),
        )

    z_half = Z_TOTAL // 2

    def z1_copies(t):
        return (
            send(spec_z.at[t, z_far, 0:z_half], z1_in.at[t, 0], z1_s.at[t, 0], z1_r.at[t, 0], lat_dev(x, z_up)),
            send(spec_z.at[t, z_far, z_half:Z_TOTAL], z1_in.at[t, 1], z1_s.at[t, 1], z1_r.at[t, 1], lat_dev(x, z_down)),
        )

    def z2_copies(t):
        return (
            send(spec_z.at[t, z_up], z2_in.at[t, 0], z2_s.at[t, 0], z2_r.at[t, 0], lat_dev(x, z_up)),
            send(spec_z.at[t, z_down], z2_in.at[t, 1], z2_s.at[t, 1], z2_r.at[t, 1], lat_dev(x, z_down)),
        )

    def x1_copies(t):
        return (
            send(spec_x.at[t, x_far, 0:2], x1_in.at[t, 0], x1_s.at[t, 0], x1_r.at[t, 0], lat_dev(x_up, z)),
            send(spec_x.at[t, x_far, 2:4], x1_in.at[t, 1], x1_s.at[t, 1], x1_r.at[t, 1], lat_dev(x_down, z)),
        )

    def x2_copies(t):
        return (
            send(spec_x.at[t, x_up], x2_in.at[t, 0], x2_s.at[t, 0], x2_r.at[t, 0], lat_dev(x_up, z)),
            send(spec_x.at[t, x_down], x2_in.at[t, 1], x2_s.at[t, 1], x2_r.at[t, 1], lat_dev(x_down, z)),
        )

    def zx_copy(t, source, to):
        n, first = Z_UNITS[to], Z_OFFSETS[to]
        return send(
            spec_z.at[t, z, first : first + n], zx_in.at[t, source, 0:n], zx_s.at[t, to], zx_r.at[t, source], lat_dev(to, z)
        )

    def xz_copies(t):
        copies = []
        for step in range(1, 4):
            to = lax.rem(z + step, 4)
            copies.append(
                send(spec_x.at[t, x, to], xz_in.at[t, step - 1], xz_s.at[t, step - 1], xz_r.at[t, step - 1], lat_dev(x, to))
            )
        return copies

    grid_copy(0).start()
    table_copy(0).start()
    grid_copy(1).start()
    for i in range(2):
        leg_copy(i).start()
    for i in range(1, CHUNKS):
        table_copy(i).start()

    barrier = pltpu.get_barrier_semaphore()
    neighbours = [lon_dev(y, 1 - core), lon_dev(y_up, core), lon_dev(y_down, core)]
    neighbours += [lat_dev(x, to) for to in (z_up, z_far, z_down)] + [lat_dev(to, z) for to in (x_up, x_far, x_down)]
    for dev in neighbours:
        pl.semaphore_signal(barrier, inc=1, device_id=dev, device_id_type=pl.DeviceIdType.MESH)

    def fields(level):
        grid_copy(level).wait()

        def rows16(block, carry):
            first = pl.multiple_of(block * 16, 16)
            for lane in range(4):
                lanes = pl.ds(lane * 128, 128)
                north, south = (
                    tendencies([grid[level, f, h, pl.ds(first, 16), lanes].astype(jnp.float32) for f in range(12)])
                    for h in range(2)
                )
                for t in range(8):
                    mix[lane * 8 + t, pl.ds(0, 16, stride=2), :] = north[t] + south[t]
                    mix[lane * 8 + t, pl.ds(1, 16, stride=2), :] = north[t] - south[t]
                for t in range(8):
                    high, low = split_bf16(mix[lane * 8 + t])
                    at = pl.multiple_of(t * 128 + block * 32, 32)
                    t_hi[level, pl.ds(at, 32), lanes] = high
                    t_lo[level, pl.ds(at, 32), lanes] = low
            return carry

        lax.fori_loop(0, 4, rows16, 0)

    fields(0)
    pl.semaphore_wait(barrier, len(neighbours))

    def analyse(t):
        slot, i, level = lax.rem(t, 2), t // LEVELS, lax.rem(t, LEVELS)

        @pl.when(level == 0)
        def _():
            table_copy(i).wait()

            def rotate(block, carry):
                q = 2 * lax.rem(block, 4) + block // 4
                c, s = eighth_cos(r * q), eighth_cos(r * q + 6)
                real, imag = table[i, block, 0], table[i, block, 1]
                for part_index, value in enumerate((real * c + imag * s, imag * c - real * s)):
                    high, low = split_bf16(value)
                    at = pl.multiple_of(block * 32 + part_index * 16, 16)
                    phases[pl.ds(at, 16), :] = high
                    phases[pl.ds(at + 256, 16), :] = low
                return carry

            lax.fori_loop(0, 8, rotate, 0)

        @pl.when(t >= 2)
        def _():
            core_copy(t - 2).wait_send()

        for n in range(ROWS // 256):
            rows = pl.ds(n * 256, 256)
            both = lax.dot_general(phases[...], t_hi[level, rows, :], NT, preferred_element_type=jnp.float32)
            rest = lax.dot_general(phases[0:256, :], t_lo[level, rows, :], NT, preferred_element_type=jnp.float32)
            value = both[0:256] + (both[256:512] + rest)
            part[slot, :, :, :, :, rows] = value.reshape(2, 4, 2, 16, 256)
        core_copy(t).start()

    def pair_sum(t):
        slot = lax.rem(t, 2)
        core_copy(t).wait_recv()

        def add(n, carry):
            yy = lax.rem(y_far + n, 4)
            paired[t, yy] = paired[t, yy] + part[slot, core, yy]
            return carry

        lax.fori_loop(0, 4, add, 0)
        for copy in y1_copies(t):
            copy.start()

    def y_forward(t):
        for copy in y1_copies(t):
            copy.wait_recv()
        paired[t, y_up, 0] = paired[t, y_up, 0] + y1_in[t, 0]
        paired[t, y_down, 1] = paired[t, y_down, 1] + y1_in[t, 1]
        for copy in y2_copies(t):
            copy.start()

    def project(t):
        i, level = t // LEVELS, lax.rem(t, LEVELS)
        slot = lax.rem(i, 2)
        for copy in y2_copies(t):
            copy.wait_recv()
        for c in range(2):
            for f in range(8):
                lanes = pl.ds(f * 128, 128)
                value = paired[t, y, c, :, lanes] + (y2_in[t, 0, c, :, lanes] + y2_in[t, 1, c, :, lanes])
                fold[pl.ds(c * 8 + f, 16, stride=16), :] = value

        @pl.when(level == 0)
        def _():
            leg_copy(i).wait()

        even = lax.rem(lax.broadcasted_iota(jnp.int32, (16, 128), 1), 2) == 0
        for owner in range(LAT_DEV):
            ox, oz = owner // 4, owner % 4
            rows = fold[owner * 16 : owner * 16 + 16, :]
            zero = jnp.zeros_like(rows)
            left = jnp.concatenate([jnp.where(even, rows, zero), jnp.where(even, zero, rows)], 0).astype(jnp.bfloat16)
            n = UNITS[ox]
            right = leg[slot, owner, :, :, 0 : 128 * n].reshape(128, 128 * n)
            value = jnp.dot(left, right, preferred_element_type=jnp.float32)
            for unit in range(n - 1):
                spec_z[t, oz, Z_OFFSETS[ox] + unit] = value[:, unit * 128 : unit * 128 + 128]
            spec_x[t, ox, oz] = value[:, (n - 1) * 128 : n * 128]
        for copy in (*z1_copies(t), *x1_copies(t)):
            copy.start()

        @pl.when((level == LEVELS - 1) & (i + 2 < CHUNKS))
        def _():
            leg_copy(i + 2).start()

    def forward(t):
        for copy in z1_copies(t):
            copy.wait_recv()
        spec_z[t, z_up, 0:z_half] = spec_z[t, z_up, 0:z_half] + z1_in[t, 0]
        spec_z[t, z_down, z_half:Z_TOTAL] = spec_z[t, z_down, z_half:Z_TOTAL] + z1_in[t, 1]
        for copy in z2_copies(t):
            copy.start()
        for copy in x1_copies(t):
            copy.wait_recv()
        spec_x[t, x_up, 0:2] = spec_x[t, x_up, 0:2] + x1_in[t, 0]
        spec_x[t, x_down, 2:4] = spec_x[t, x_down, 2:4] + x1_in[t, 1]
        for copy in x2_copies(t):
            copy.start()

    def cross(t):
        for copy in z2_copies(t):
            copy.wait_recv()
        spec_z[t, z] = spec_z[t, z] + (z2_in[t, 0] + z2_in[t, 1])
        for to in range(3):

            @pl.when(x != to)
            def _():
                zx_copy(t, x, to).start()

        for copy in x2_copies(t):
            copy.wait_recv()
        spec_x[t, x] = spec_x[t, x] + (x2_in[t, 0] + x2_in[t, 1])
        for copy in xz_copies(t):
            copy.start()

    def finish(t):
        i, level = t // LEVELS, lax.rem(t, LEVELS)
        order = r + LON_DEV * (CHUNKS * k + i)
        lane = lax.broadcasted_iota(jnp.int32, (16, 128), 1)
        for copy in xz_copies(t):
            copy.wait_recv()

        def write(unit, e, value):
            inside = order + 2 * (lane + unit * 128) + e < WAVES
            out_ref[i, level, :, pl.ds(e * 512 + unit * 128, 128)] = jnp.where(inside, value, jnp.zeros_like(value))

        for mine in range(4):

            @pl.when(x == mine)
            def _():
                n, first = Z_UNITS[mine], Z_OFFSETS[mine]
                others = [source for source in range(4) if source != mine]
                for source in others if n else ():
                    zx_copy(t, source, mine).wait_recv()
                for e in range(2):
                    rows = pl.ds(e * 16, 16)
                    for unit in range(n):
                        value = spec_z[t, z, first + unit, rows, :]
                        for source in others:
                            value = value + zx_in[t, source, unit, rows, :]
                        write(unit, e, value)
                    value = spec_x[t, mine, z, rows, :]
                    for step in range(3):
                        value = value + xz_in[t, step, rows, :]
                    write(n, e, value)
                    for unit in range(n + 1, 4):
                        out_ref[i, level, :, pl.ds(e * 512 + unit * 128, 128)] = jnp.zeros((16, 128), jnp.float32)

    def stage(run, t):
        @pl.when((t >= 0) & (t < STEPS))
        def _():
            run(t)

    def steps(step, carry):
        t = step - 3
        stage(y_forward, t)
        stage(project, t - 1)
        stage(forward, t - 2)
        stage(cross, t - 3)
        stage(finish, t - 4)
        stage(pair_sum, t + 2)

        @pl.when(t == -2)
        def _():
            fields(1)

        stage(analyse, t + 3)
        return carry

    lax.fori_loop(0, STEPS + 7, steps, 0)

    def drain(t, carry):
        @pl.when(t >= STEPS - 2)
        def _():
            core_copy(t).wait_send()

        ring = (*y1_copies(t), *y2_copies(t), *z1_copies(t), *z2_copies(t), *x1_copies(t), *x2_copies(t))
        for copy in (*ring, *xz_copies(t)):
            copy.wait_send()
        for to in range(3):

            @pl.when(x != to)
            def _():
                zx_copy(t, x, to).wait_send()

        return carry

    lax.fori_loop(0, STEPS, drain, 0)


def local(grid, legendre):
    table = jnp.asarray(phase_table())
    f32, bf16 = jnp.float32, jnp.bfloat16
    dma = pltpu.SemaphoreType.DMA
    result = pl.pallas_call(
        kernel,
        out_shape=jax.ShapeDtypeStruct((CHUNKS, LEVELS, 16, WAVES), f32),
        in_specs=[pl.BlockSpec(memory_space=pl.ANY)] * 3,
        out_specs=pl.BlockSpec(memory_space=pltpu.VMEM),
        scratch_shapes=[
            pltpu.VMEM((LEVELS, 12, 2, 64, LON_LOCAL), bf16),
            pltpu.VMEM((LEVELS, ROWS, LON_LOCAL), bf16),
            pltpu.VMEM((LEVELS, ROWS, LON_LOCAL), bf16),
            pltpu.VMEM((32, 32, 128), f32),
            pltpu.VMEM((CHUNKS, 8, 2, 16, LON_LOCAL), f32),
            pltpu.VMEM((512, LON_LOCAL), bf16),
            pltpu.VMEM((2, 2, 4, 2, 16, ROWS), f32),
            pltpu.VMEM((STEPS, 4, 2, 16, ROWS), f32),
            pltpu.VMEM((STEPS, 2, 16, ROWS), f32),
            pltpu.VMEM((STEPS, 2, 2, 16, ROWS), f32),
            pltpu.VMEM((256, 128), f32),
            pltpu.VMEM((2, 16, 64, 2, 512), bf16),
            pltpu.VMEM((STEPS, 4, Z_TOTAL, 32, 128), f32),
            pltpu.VMEM((STEPS, 4, 4, 32, 128), f32),
            pltpu.VMEM((STEPS, 2, Z_TOTAL // 2, 32, 128), f32),
            pltpu.VMEM((STEPS, 2, Z_TOTAL, 32, 128), f32),
            pltpu.VMEM((STEPS, 4, 3, 32, 128), f32),
            pltpu.VMEM((STEPS, 2, 2, 32, 128), f32),
            pltpu.VMEM((STEPS, 2, 4, 32, 128), f32),
            pltpu.VMEM((STEPS, 3, 32, 128), f32),
            dma((LEVELS,)),
            dma((CHUNKS,)),
            dma((2,)),
            dma((STEPS,)),
            dma((STEPS,)),
            *[dma((STEPS, 2)) for _ in range(12)],
            *[dma((STEPS, 4)) for _ in range(2)],
            *[dma((STEPS, 3)) for _ in range(2)],
        ],
        compiler_params=pltpu.CompilerParams(
            collective_id=0, has_side_effects=True, vmem_limit_bytes=62 * 2**20
        ),
        name="spectral",
    )(grid, table, legendre.reshape(LAT_DEV, CHUNKS, 64, 2, 512))
    spectral = result.reshape(1, CHUNKS, LEVELS, 2, 8, 2, WAVES // 2)
    return jnp.transpose(spectral, (0, 1, 4, 2, 3, 5, 6))


def solution(mesh):
    in_specs = (P(None, None, None, "lat", "lon"), P("lon", None, "lat", None, None))
    out_specs = P("lon", "lat", None, None, None, None, None)
    return jax.shard_map(local, mesh=mesh, in_specs=in_specs, out_specs=out_specs, check_vma=False)
```

```python
import jax
import jax.numpy as jnp
import numpy as np
from jax import lax
from jax.experimental import pallas as pl
from jax.experimental.pallas import tpu as pltpu
from jax.sharding import PartitionSpec as P

NLON = 4096
WAVES = 1024
LON_DEV = 8
LAT_DEV = 16
LON_LOCAL = NLON // LON_DEV
ROWS = 1024
CHUNKS = 8
LEVELS = 2
STEPS = CHUNKS * LEVELS
UNITS = (4, 3, 2, 1)
Z_UNITS = (3, 2, 1, 0)
Z_OFFSETS = (0, 3, 5, 6)
Z_TOTAL = 6
X_ROWS = (32, 32, 16, 16)
X_OFFSETS = (0, 32, 64, 80)
X_TOTAL = 96
X_HALF = X_TOTAL // 2
ADIABATIC = 0.286
ROOT_HALF = 0.5**0.5


def phase_table():
    i, core, y, k = np.meshgrid(
        np.arange(CHUNKS), np.arange(2), np.arange(4), np.arange(LAT_DEV), indexing="ij"
    )
    m = 2 * y + core + LON_DEV * (CHUNKS * k + i)
    turns = m[..., None] * np.arange(LON_LOCAL) % NLON
    angles = turns * (2.0 * np.pi / NLON)
    table = np.stack([np.cos(angles), -np.sin(angles)], 3) / np.sqrt(NLON)
    return table.reshape(CHUNKS, 8, 2, LAT_DEV, LON_LOCAL).astype(np.float32)


def eighth_cos(n):
    n = lax.rem(n, 8)
    value = jnp.float32(1.0)
    for at, root in ((1, ROOT_HALF), (2, 0.0), (3, -ROOT_HALF), (4, -1.0), (5, -ROOT_HALF), (6, 0.0), (7, ROOT_HALF)):
        value = jnp.where(n == at, jnp.float32(root), value)
    return value


def tendencies(f):
    u, v, zeta, div, temp, hum, temp_x, temp_y, hum_x, hum_y, press_x, press_y = f
    return (
        zeta * v - temp * press_x,
        -zeta * u - temp * press_y,
        u * v,
        -(u * temp_x + v * temp_y) + ADIABATIC * temp * div,
        -(u * hum_x + v * hum_y) - hum * div,
        u * temp,
        v * temp,
        v * hum,
    )


def split_bf16(a):
    high = a.astype(jnp.bfloat16)
    return high, (a - high.astype(jnp.float32)).astype(jnp.bfloat16)


NT = (((1,), (1,)), ((), ()))


def kernel(
    grid_ref, table_ref, leg_ref, out_ref,
    grid, t_hi, t_lo, mix, table, phases, part, paired, y1_in, y2_in, fold, leg,
    spec_z, spec_x, z1_in, z2_in, zx_in, x1_in, x2_in, xz_in, result,
    grid_sem, out_sem, table_sem, leg_sem, core_s, core_r, y1_s, y1_r, y2_s, y2_r,
    z1_s, z1_r, z2_s, z2_r, x1_s, x1_r, x2_s, x2_r, zx_s, zx_r, xz_s, xz_r,
):
    r = lax.axis_index("lon")
    k = lax.axis_index("lat")
    y, core = r // 2, lax.rem(r, 2)
    x, z = k // 4, lax.rem(k, 4)
    y_up, y_down = lax.rem(y + 1, 4), lax.rem(y + 3, 4)
    z_up, z_down = lax.rem(z + 1, 4), lax.rem(z + 3, 4)
    x_up, x_down = lax.rem(x + 1, 4), lax.rem(x + 3, 4)
    x_far, y_far, z_far = lax.rem(x + 2, 4), lax.rem(y + 2, 4), lax.rem(z + 2, 4)

    def lon_dev(yy, cc):
        return {"lon": yy * 2 + cc}

    def lat_dev(xx, zz):
        return {"lat": xx * 4 + zz}

    def send(src, dst, s, q, dev):
        return pltpu.make_async_remote_copy(
            src_ref=src, dst_ref=dst, send_sem=s, recv_sem=q, device_id=dev, device_id_type=pl.DeviceIdType.MESH
        )

    def table_copy(t):
        return pltpu.make_async_copy(table_ref.at[t], table.at[t], table_sem.at[t])

    def leg_copy(t):
        slot = lax.rem(t, 2)
        return pltpu.make_async_copy(leg_ref.at[:, lax.rem(t, CHUNKS)], leg.at[slot], leg_sem.at[slot])

    def out_copy(t):
        at = (lax.rem(t, CHUNKS), t // CHUNKS)
        return pltpu.make_async_copy(result.at[at], out_ref.at[at], out_sem.at[t])

    def grid_copy(level):
        return pltpu.make_async_copy(grid_ref.at[:, level], grid.at[level], grid_sem.at[level])

    def core_copy(t):
        return send(
            part.at[lax.rem(t, 2), 1 - core], paired.at[t], core_s.at[t], core_r.at[t], lon_dev(y, 1 - core)
        )

    def y1_copies(t):
        return (
            send(paired.at[t, y_far, 0], y1_in.at[t, 0], y1_s.at[t, 0], y1_r.at[t, 0], lon_dev(y_up, core)),
            send(paired.at[t, y_far, 1], y1_in.at[t, 1], y1_s.at[t, 1], y1_r.at[t, 1], lon_dev(y_down, core)),
        )

    def y2_copies(t):
        return (
            send(paired.at[t, y_up], y2_in.at[t, 0], y2_s.at[t, 0], y2_r.at[t, 0], lon_dev(y_up, core)),
            send(paired.at[t, y_down], y2_in.at[t, 1], y2_s.at[t, 1], y2_r.at[t, 1], lon_dev(y_down, core)),
        )

    z_half = Z_TOTAL // 2

    def z1_copies(t):
        return (
            send(spec_z.at[t, z_far, 0:z_half], z1_in.at[t, 0], z1_s.at[t, 0], z1_r.at[t, 0], lat_dev(x, z_up)),
            send(spec_z.at[t, z_far, z_half:Z_TOTAL], z1_in.at[t, 1], z1_s.at[t, 1], z1_r.at[t, 1], lat_dev(x, z_down)),
        )

    def z2_copies(t):
        return (
            send(spec_z.at[t, z_up], z2_in.at[t, 0], z2_s.at[t, 0], z2_r.at[t, 0], lat_dev(x, z_up)),
            send(spec_z.at[t, z_down], z2_in.at[t, 1], z2_s.at[t, 1], z2_r.at[t, 1], lat_dev(x, z_down)),
        )

    def x1_copies(t):
        return (
            send(spec_x.at[t, x_far, 0:X_HALF], x1_in.at[t, 0], x1_s.at[t, 0], x1_r.at[t, 0], lat_dev(x_up, z)),
            send(spec_x.at[t, x_far, X_HALF:X_TOTAL], x1_in.at[t, 1], x1_s.at[t, 1], x1_r.at[t, 1], lat_dev(x_down, z)),
        )

    def x2_copies(t):
        return (
            send(spec_x.at[t, x_up], x2_in.at[t, 0], x2_s.at[t, 0], x2_r.at[t, 0], lat_dev(x_up, z)),
            send(spec_x.at[t, x_down], x2_in.at[t, 1], x2_s.at[t, 1], x2_r.at[t, 1], lat_dev(x_down, z)),
        )

    def zx_copy(t, source, to):
        n, first = Z_UNITS[to], Z_OFFSETS[to]
        return send(
            spec_z.at[t, z, first : first + n], zx_in.at[t, source, 0:n], zx_s.at[t, to], zx_r.at[t, source], lat_dev(to, z)
        )

    def xz_copy(t, source, to):
        n, first = X_ROWS[to], X_OFFSETS[to]
        return send(
            spec_x.at[t, x, first : first + n], xz_in.at[t, source, 0:n], xz_s.at[t, to], xz_r.at[t, source], lat_dev(x, to)
        )

    table_copy(0).start()
    grid_copy(0).start()
    grid_copy(1).start()
    for i in range(2):
        leg_copy(i).start()
    for i in range(1, CHUNKS):
        table_copy(i).start()

    barrier = pltpu.get_barrier_semaphore()
    neighbours = [lon_dev(y, 1 - core), lon_dev(y_up, core), lon_dev(y_down, core)]
    neighbours += [lat_dev(x, to) for to in (z_up, z_far, z_down)] + [lat_dev(to, z) for to in (x_up, x_far, x_down)]
    for dev in neighbours:
        pl.semaphore_signal(barrier, inc=1, device_id=dev, device_id_type=pl.DeviceIdType.MESH)

    def fields(level):
        grid_copy(level).wait()

        def rows16(block, carry):
            first = pl.multiple_of(block * 16, 16)
            for lane in range(4):
                lanes = pl.ds(lane * 128, 128)
                north, south = (
                    tendencies([grid[level, f, h, pl.ds(first, 16), lanes].astype(jnp.float32) for f in range(12)])
                    for h in range(2)
                )
                for t in range(8):
                    mix[lane * 8 + t, pl.ds(0, 16, stride=2), :] = north[t] + south[t]
                    mix[lane * 8 + t, pl.ds(1, 16, stride=2), :] = north[t] - south[t]
                for t in range(8):
                    high, low = split_bf16(mix[lane * 8 + t])
                    at = pl.multiple_of(t * 128 + block * 32, 32)
                    t_hi[level, pl.ds(at, 32), lanes] = high
                    t_lo[level, pl.ds(at, 32), lanes] = low
            return carry

        lax.fori_loop(0, 4, rows16, 0)

    def rotate(t):
        i = lax.rem(t, CHUNKS)

        @pl.when(t < CHUNKS)
        def _():
            table_copy(i).wait()

        def block_of(block, carry):
            q = 2 * lax.rem(block, 4) + block // 4
            c, s = eighth_cos(r * q), eighth_cos(r * q + 6)
            real, imag = table[i, block, 0], table[i, block, 1]
            for part_index, value in enumerate((real * c + imag * s, imag * c - real * s)):
                high, low = split_bf16(value)
                at = pl.multiple_of(block * 32 + part_index * 16, 16)
                phases[pl.ds(at, 16), :] = high
                phases[pl.ds(at + 256, 16), :] = low
            return carry

        lax.fori_loop(0, 8, block_of, 0)

    rotate(0)
    fields(0)

    pl.semaphore_wait(barrier, len(neighbours))

    def analyse(t):
        slot, level = lax.rem(t, 2), t // CHUNKS

        @pl.when(t >= 2)
        def _():
            core_copy(t - 2).wait_send()

        for n in range(ROWS // 256):
            rows = pl.ds(n * 256, 256)
            both = lax.dot_general(phases[...], t_hi[level, rows, :], NT, preferred_element_type=jnp.float32)
            rest = lax.dot_general(phases[0:256, :], t_lo[level, rows, :], NT, preferred_element_type=jnp.float32)
            value = both[0:256] + (both[256:512] + rest)
            part[slot, :, :, :, :, rows] = value.reshape(2, 4, 2, 16, 256)
        core_copy(t).start()

        @pl.when(t + 1 < STEPS)
        def _():
            rotate(t + 1)

    def pair_sum(t):
        slot = lax.rem(t, 2)
        core_copy(t).wait_recv()

        def add(n, carry):
            yy = lax.rem(y_far + n, 4)
            paired[t, yy] = paired[t, yy] + part[slot, core, yy]
            return carry

        lax.fori_loop(0, 4, add, 0)
        for copy in y1_copies(t):
            copy.start()

    def y_forward(t):
        for copy in y1_copies(t):
            copy.wait_recv()
        paired[t, y_up, 0] = paired[t, y_up, 0] + y1_in[t, 0]
        paired[t, y_down, 1] = paired[t, y_down, 1] + y1_in[t, 1]
        for copy in y2_copies(t):
            copy.start()

    def project(t):
        slot = lax.rem(t, 2)
        for copy in y2_copies(t):
            copy.wait_recv()
        for c in range(2):
            for f in range(8):
                lanes = pl.ds(f * 128, 128)
                value = paired[t, y, c, :, lanes] + (y2_in[t, 0, c, :, lanes] + y2_in[t, 1, c, :, lanes])
                fold[pl.ds(c * 8 + f, 16, stride=16), :] = value

        leg_copy(t).wait()
        lane = lax.broadcasted_iota(jnp.int32, (16, 128), 1)
        even, low_half = lax.rem(lane, 2) == 0, lane < 64
        for owner in range(LAT_DEV):
            ox, oz = owner // 4, owner % 4
            rows = fold[owner * 16 : owner * 16 + 16, :]
            zero = jnp.zeros_like(rows)
            left = jnp.concatenate([jnp.where(even, rows, zero), jnp.where(even, zero, rows)], 0).astype(jnp.bfloat16)
            n = UNITS[ox]
            right = leg[slot, owner, :, :, 0 : 128 * n].reshape(128, 128 * n)
            value = jnp.dot(left, right, preferred_element_type=jnp.float32)
            for unit in range(n - 1):
                spec_z[t, oz, Z_OFFSETS[ox] + unit] = value[:, unit * 128 : unit * 128 + 128]
            last, first = value[:, (n - 1) * 128 : n * 128], X_OFFSETS[oz]
            if X_ROWS[oz] == 32:
                spec_x[t, ox, first : first + 32, :] = last
            else:
                spec_x[t, ox, first : first + 16, :] = jnp.where(low_half, last[0:16], pltpu.roll(last[16:32], 64, 1))
        for copy in (*z1_copies(t), *x1_copies(t)):
            copy.start()

        @pl.when(t + 2 < STEPS)
        def _():
            leg_copy(t + 2).start()

    def forward(t):
        for copy in z1_copies(t):
            copy.wait_recv()
        spec_z[t, z_up, 0:z_half] = spec_z[t, z_up, 0:z_half] + z1_in[t, 0]
        spec_z[t, z_down, z_half:Z_TOTAL] = spec_z[t, z_down, z_half:Z_TOTAL] + z1_in[t, 1]
        for copy in z2_copies(t):
            copy.start()
        for copy in x1_copies(t):
            copy.wait_recv()
        spec_x[t, x_up, 0:X_HALF] = spec_x[t, x_up, 0:X_HALF] + x1_in[t, 0]
        spec_x[t, x_down, X_HALF:X_TOTAL] = spec_x[t, x_down, X_HALF:X_TOTAL] + x1_in[t, 1]
        for copy in x2_copies(t):
            copy.start()

    def cross(t):
        for copy in z2_copies(t):
            copy.wait_recv()
        spec_z[t, z] = spec_z[t, z] + (z2_in[t, 0] + z2_in[t, 1])
        for to in range(3):

            @pl.when(x != to)
            def _():
                zx_copy(t, x, to).start()

        for copy in x2_copies(t):
            copy.wait_recv()
        spec_x[t, x] = spec_x[t, x] + (x2_in[t, 0] + x2_in[t, 1])
        for to in range(4):

            @pl.when(z != to)
            def _():
                xz_copy(t, z, to).start()

    def finish(t):
        i, level = lax.rem(t, CHUNKS), t // CHUNKS
        order = r + LON_DEV * (CHUNKS * k + i)
        lane = lax.broadcasted_iota(jnp.int32, (16, 128), 1)
        def write(unit, e, value):
            inside = order + 2 * (lane + unit * 128) + e < WAVES
            first = e * 512 + unit * 128
            first = first if isinstance(first, int) else pl.multiple_of(first, 128)
            result[i, level, :, pl.ds(first, 128)] = jnp.where(inside, value, jnp.zeros_like(value))

        for mine in range(4):

            @pl.when(x == mine)
            def _():
                n, first = Z_UNITS[mine], Z_OFFSETS[mine]
                others = [source for source in range(4) if source != mine]
                for source in others if n else ():
                    zx_copy(t, source, mine).wait_recv()
                for e in range(2):
                    rows = pl.ds(e * 16, 16)
                    for unit in range(n):
                        value = spec_z[t, z, first + unit, rows, :]
                        for source in others:
                            value = value + zx_in[t, source, unit, rows, :]
                        write(unit, e, value)
                    for unit in range(n + 1, 4):
                        result[i, level, :, pl.ds(e * 512 + unit * 128, 128)] = jnp.zeros((16, 128), jnp.float32)

        for mine in range(4):

            @pl.when(z == mine)
            def _():
                n, first = X_ROWS[mine], X_OFFSETS[mine]
                others = [source for source in range(4) if source != mine]
                for source in others:
                    xz_copy(t, source, mine).wait_recv()
                value = spec_x[t, x, first : first + n, :]
                for source in others:
                    value = value + xz_in[t, source, 0:n, :]
                write(3 - x, 0, value[0:16])
                write(3 - x, 1, value[16:32] if n == 32 else pltpu.roll(value, 64, 1))

        out_copy(t).start()

    def stage(run, t):
        @pl.when((t >= 0) & (t < STEPS))
        def _():
            run(t)

    def steps(step, carry):
        t = step - 4
        stage(y_forward, t)
        stage(project, t - 1)
        stage(forward, t - 2)
        stage(cross, t - 3)
        stage(pair_sum, t + 2)
        stage(finish, t - 4)
        stage(analyse, t + 4)

        @pl.when(t == 0)
        def _():
            fields(1)

        return carry

    lax.fori_loop(0, STEPS + 8, steps, 0)

    def drain(t, carry):
        @pl.when(t >= STEPS - 2)
        def _():
            core_copy(t).wait_send()

        ring = (*y1_copies(t), *y2_copies(t), *z1_copies(t), *z2_copies(t), *x1_copies(t), *x2_copies(t))
        for copy in ring:
            copy.wait_send()
        out_copy(t).wait()
        for to in range(4):

            @pl.when(z != to)
            def _():
                xz_copy(t, z, to).wait_send()

        for to in range(3):

            @pl.when(x != to)
            def _():
                zx_copy(t, x, to).wait_send()

        return carry

    lax.fori_loop(0, STEPS, drain, 0)


def local(grid, legendre):
    table = jnp.asarray(phase_table())
    f32, bf16 = jnp.float32, jnp.bfloat16
    dma = pltpu.SemaphoreType.DMA
    result = pl.pallas_call(
        kernel,
        out_shape=jax.ShapeDtypeStruct((CHUNKS, LEVELS, 16, WAVES), f32),
        in_specs=[pl.BlockSpec(memory_space=pl.ANY)] * 3,
        out_specs=pl.BlockSpec(memory_space=pl.ANY),
        scratch_shapes=[
            pltpu.VMEM((LEVELS, 12, 2, 64, LON_LOCAL), bf16),
            pltpu.VMEM((LEVELS, ROWS, LON_LOCAL), bf16),
            pltpu.VMEM((LEVELS, ROWS, LON_LOCAL), bf16),
            pltpu.VMEM((32, 32, 128), f32),
            pltpu.VMEM((CHUNKS, 8, 2, 16, LON_LOCAL), f32),
            pltpu.VMEM((512, LON_LOCAL), bf16),
            pltpu.VMEM((2, 2, 4, 2, 16, ROWS), f32),
            pltpu.VMEM((STEPS, 4, 2, 16, ROWS), f32),
            pltpu.VMEM((STEPS, 2, 16, ROWS), f32),
            pltpu.VMEM((STEPS, 2, 2, 16, ROWS), f32),
            pltpu.VMEM((256, 128), f32),
            pltpu.VMEM((2, 16, 64, 2, 512), bf16),
            pltpu.VMEM((STEPS, 4, Z_TOTAL, 32, 128), f32),
            pltpu.VMEM((STEPS, 4, X_TOTAL, 128), f32),
            pltpu.VMEM((STEPS, 2, Z_TOTAL // 2, 32, 128), f32),
            pltpu.VMEM((STEPS, 2, Z_TOTAL, 32, 128), f32),
            pltpu.VMEM((STEPS, 4, 3, 32, 128), f32),
            pltpu.VMEM((STEPS, 2, X_HALF, 128), f32),
            pltpu.VMEM((STEPS, 2, X_TOTAL, 128), f32),
            pltpu.VMEM((STEPS, 4, 32, 128), f32),
            pltpu.VMEM((CHUNKS, LEVELS, 16, WAVES), f32),
            dma((LEVELS,)),
            dma((STEPS,)),
            dma((CHUNKS,)),
            dma((2,)),
            dma((STEPS,)),
            dma((STEPS,)),
            *[dma((STEPS, 2)) for _ in range(12)],
            *[dma((STEPS, 4)) for _ in range(4)],
        ],
        compiler_params=pltpu.CompilerParams(
            collective_id=0, has_side_effects=True, vmem_limit_bytes=62 * 2**20
        ),
        name="spectral",
    )(grid, table, legendre.reshape(LAT_DEV, CHUNKS, 64, 2, 512))
    spectral = result.reshape(1, CHUNKS, LEVELS, 2, 8, 2, WAVES // 2)
    return jnp.transpose(spectral, (0, 1, 4, 2, 3, 5, 6))


def solution(mesh):
    in_specs = (P(None, None, None, "lat", "lon"), P("lon", None, "lat", None, None))
    out_specs = P("lon", "lat", None, None, None, None, None)
    return jax.shard_map(local, mesh=mesh, in_specs=in_specs, out_specs=out_specs, check_vma=False)
```

```python
import jax
import jax.numpy as jnp
import numpy as np
from jax import lax
from jax.experimental import pallas as pl
from jax.experimental.pallas import tpu as pltpu
from jax.sharding import PartitionSpec as P

NLON = 4096
WAVES = 1024
LON_DEV = 8
LAT_DEV = 16
LON_LOCAL = NLON // LON_DEV
ROWS = 1024
CHUNKS = 8
LEVELS = 2
STEPS = CHUNKS * LEVELS
UNITS = (4, 3, 2, 1)
Z_UNITS = (3, 2, 1, 0)
Z_OFFSETS = (0, 3, 5, 6)
Z_TOTAL = 6
X_ROWS = (32, 32, 16, 16)
X_OFFSETS = (0, 32, 64, 80)
X_TOTAL = 96
X_HALF = X_TOTAL // 2
ADIABATIC = 0.286
ROOT_HALF = 0.5**0.5


def phase_table():
    i, core, y, k = np.meshgrid(
        np.arange(CHUNKS), np.arange(2), np.arange(4), np.arange(LAT_DEV), indexing="ij"
    )
    m = 2 * y + core + LON_DEV * (CHUNKS * k + i)
    turns = m[..., None] * np.arange(LON_LOCAL) % NLON
    angles = turns * (2.0 * np.pi / NLON)
    table = np.stack([np.cos(angles), -np.sin(angles)], 3) / np.sqrt(NLON)
    return table.reshape(CHUNKS, 8, 2, LAT_DEV, LON_LOCAL).astype(np.float32)


def eighth_cos(n):
    n = lax.rem(n, 8)
    value = jnp.float32(1.0)
    for at, root in ((1, ROOT_HALF), (2, 0.0), (3, -ROOT_HALF), (4, -1.0), (5, -ROOT_HALF), (6, 0.0), (7, ROOT_HALF)):
        value = jnp.where(n == at, jnp.float32(root), value)
    return value


def tendencies(f):
    u, v, zeta, div, temp, hum, temp_x, temp_y, hum_x, hum_y, press_x, press_y = f
    return (
        zeta * v - temp * press_x,
        -zeta * u - temp * press_y,
        u * v,
        -(u * temp_x + v * temp_y) + ADIABATIC * temp * div,
        -(u * hum_x + v * hum_y) - hum * div,
        u * temp,
        v * temp,
        v * hum,
    )


def split_bf16(a):
    high = a.astype(jnp.bfloat16)
    return high, (a - high.astype(jnp.float32)).astype(jnp.bfloat16)


NT = (((1,), (1,)), ((), ()))


def kernel(
    grid_ref, table_ref, leg_ref, out_ref,
    grid, t_hi, t_lo, mix, table, phases, part, paired, y1_in, y2_in, fold, leg,
    spec_z, spec_x, z1_in, z2_in, zx_in, x1_in, x2_in, xz_in, result,
    grid_sem, out_sem, table_sem, leg_sem, core_s, core_r, y1_s, y1_r, y2_s, y2_r,
    z1_s, z1_r, z2_s, z2_r, x1_s, x1_r, x2_s, x2_r, zx_s, zx_r, xz_s, xz_r,
):
    r = lax.axis_index("lon")
    k = lax.axis_index("lat")
    y, core = r // 2, lax.rem(r, 2)
    x, z = k // 4, lax.rem(k, 4)
    y_up, y_down = lax.rem(y + 1, 4), lax.rem(y + 3, 4)
    z_up, z_down = lax.rem(z + 1, 4), lax.rem(z + 3, 4)
    x_up, x_down = lax.rem(x + 1, 4), lax.rem(x + 3, 4)
    x_far, y_far, z_far = lax.rem(x + 2, 4), lax.rem(y + 2, 4), lax.rem(z + 2, 4)

    def lon_dev(yy, cc):
        return {"lon": yy * 2 + cc}

    def lat_dev(xx, zz):
        return {"lat": xx * 4 + zz}

    def send(src, dst, s, q, dev):
        return pltpu.make_async_remote_copy(
            src_ref=src, dst_ref=dst, send_sem=s, recv_sem=q, device_id=dev, device_id_type=pl.DeviceIdType.MESH
        )

    def arrived(ref, sem):
        pltpu.make_async_copy(ref, ref, sem).wait()

    def table_copy(t):
        return pltpu.make_async_copy(table_ref.at[t], table.at[t], table_sem.at[t])

    def leg_copy(t):
        slot = lax.rem(t, 2)
        return pltpu.make_async_copy(leg_ref.at[:, lax.rem(t, CHUNKS)], leg.at[slot], leg_sem.at[slot])

    def out_copy(t):
        at = (lax.rem(t, CHUNKS), t // CHUNKS)
        return pltpu.make_async_copy(result.at[at], out_ref.at[at], out_sem)

    def grid_copy(level):
        return pltpu.make_async_copy(grid_ref.at[:, level], grid.at[level], grid_sem.at[level])

    def core_copy(t):
        return send(
            part.at[lax.rem(t, 2), 1 - core], paired.at[t], core_s.at[t], core_r.at[t], lon_dev(y, 1 - core)
        )

    def y1_copies(t):
        return (
            send(paired.at[t, y_far, 0], y1_in.at[t, 0], y1_s.at[0], y1_r.at[t], lon_dev(y_up, core)),
            send(paired.at[t, y_far, 1], y1_in.at[t, 1], y1_s.at[1], y1_r.at[t], lon_dev(y_down, core)),
        )

    def y2_copies(t):
        return (
            send(paired.at[t, y_up], y2_in.at[t, 0], y2_s.at[0], y2_r.at[t], lon_dev(y_up, core)),
            send(paired.at[t, y_down], y2_in.at[t, 1], y2_s.at[1], y2_r.at[t], lon_dev(y_down, core)),
        )

    z_half = Z_TOTAL // 2

    def z1_copies(t):
        return (
            send(spec_z.at[t, z_far, 0:z_half], z1_in.at[t, 0], z1_s.at[0], z1_r.at[t], lat_dev(x, z_up)),
            send(spec_z.at[t, z_far, z_half:Z_TOTAL], z1_in.at[t, 1], z1_s.at[1], z1_r.at[t], lat_dev(x, z_down)),
        )

    def z2_copies(t):
        return (
            send(spec_z.at[t, z_up], z2_in.at[t, 0], z2_s.at[0], z2_r.at[t], lat_dev(x, z_up)),
            send(spec_z.at[t, z_down], z2_in.at[t, 1], z2_s.at[1], z2_r.at[t], lat_dev(x, z_down)),
        )

    def x1_copies(t):
        return (
            send(spec_x.at[t, x_far, 0:X_HALF], x1_in.at[t, 0], x1_s.at[0], x1_r.at[t], lat_dev(x_up, z)),
            send(spec_x.at[t, x_far, X_HALF:X_TOTAL], x1_in.at[t, 1], x1_s.at[1], x1_r.at[t], lat_dev(x_down, z)),
        )

    def x2_copies(t):
        return (
            send(spec_x.at[t, x_up], x2_in.at[t, 0], x2_s.at[0], x2_r.at[t], lat_dev(x_up, z)),
            send(spec_x.at[t, x_down], x2_in.at[t, 1], x2_s.at[1], x2_r.at[t], lat_dev(x_down, z)),
        )

    def zx_copy(t, source, to):
        n, first = Z_UNITS[to], Z_OFFSETS[to]
        return send(
            spec_z.at[t, z, first : first + n], zx_in.at[t, source, 0:n], zx_s.at[to], zx_r.at[t], lat_dev(to, z)
        )

    def xz_copy(t, source, to):
        n, first = X_ROWS[to], X_OFFSETS[to]
        return send(
            spec_x.at[t, x, first : first + n], xz_in.at[t, source, 0:n], xz_s.at[to], xz_r.at[t], lat_dev(x, to)
        )

    table_copy(0).start()
    grid_copy(0).start()
    grid_copy(1).start()
    for i in range(2):
        leg_copy(i).start()
    for i in range(1, CHUNKS):
        table_copy(i).start()

    barrier = pltpu.get_barrier_semaphore()
    neighbours = [lon_dev(y, 1 - core), lon_dev(y_up, core), lon_dev(y_down, core)]
    neighbours += [lat_dev(x, to) for to in (z_up, z_far, z_down)] + [lat_dev(to, z) for to in (x_up, x_far, x_down)]
    for dev in neighbours:
        pl.semaphore_signal(barrier, inc=1, device_id=dev, device_id_type=pl.DeviceIdType.MESH)

    def fields(level):
        grid_copy(level).wait()

        def rows16(block, carry):
            first = pl.multiple_of(block * 16, 16)
            for lane in range(4):
                lanes = pl.ds(lane * 128, 128)
                north, south = (
                    tendencies([grid[level, f, h, pl.ds(first, 16), lanes].astype(jnp.float32) for f in range(12)])
                    for h in range(2)
                )
                for t in range(8):
                    mix[lane * 8 + t, pl.ds(0, 16, stride=2), :] = north[t] + south[t]
                    mix[lane * 8 + t, pl.ds(1, 16, stride=2), :] = north[t] - south[t]
                for t in range(8):
                    high, low = split_bf16(mix[lane * 8 + t])
                    at = pl.multiple_of(t * 128 + block * 32, 32)
                    t_hi[level, pl.ds(at, 32), lanes] = high
                    t_lo[level, pl.ds(at, 32), lanes] = low
            return carry

        lax.fori_loop(0, 4, rows16, 0)

    def rotate(t):
        i = lax.rem(t, CHUNKS)

        @pl.when(t < CHUNKS)
        def _():
            table_copy(i).wait()

        def block_of(block, carry):
            q = 2 * lax.rem(block, 4) + block // 4
            c, s = eighth_cos(r * q), eighth_cos(r * q + 6)
            real, imag = table[i, block, 0], table[i, block, 1]
            for part_index, value in enumerate((real * c + imag * s, imag * c - real * s)):
                high, low = split_bf16(value)
                at = pl.multiple_of(block * 32 + part_index * 16, 16)
                phases[pl.ds(at, 16), :] = high
                phases[pl.ds(at + 256, 16), :] = low
            return carry

        lax.fori_loop(0, 8, block_of, 0)

    rotate(0)
    fields(0)

    pl.semaphore_wait(barrier, len(neighbours))

    def analyse(t):
        slot, level = lax.rem(t, 2), t // CHUNKS

        @pl.when(t >= 2)
        def _():
            core_copy(t - 2).wait_send()

        for n in range(ROWS // 256):
            rows = pl.ds(n * 256, 256)
            both = lax.dot_general(phases[...], t_hi[level, rows, :], NT, preferred_element_type=jnp.float32)
            rest = lax.dot_general(phases[0:256, :], t_lo[level, rows, :], NT, preferred_element_type=jnp.float32)
            value = both[0:256] + (both[256:512] + rest)
            part[slot, :, :, :, :, rows] = value.reshape(2, 4, 2, 16, 256)
        core_copy(t).start()

        @pl.when(t + 1 < STEPS)
        def _():
            rotate(t + 1)

    def pair_sum(t):
        slot = lax.rem(t, 2)
        core_copy(t).wait_recv()

        def add(n, carry):
            yy = lax.rem(y_far + n, 4)
            paired[t, yy] = paired[t, yy] + part[slot, core, yy]
            return carry

        lax.fori_loop(0, 4, add, 0)
        for copy in y1_copies(t):
            copy.start()

    def y_forward(t):
        arrived(y1_in.at[t], y1_r.at[t])
        paired[t, y_up, 0] = paired[t, y_up, 0] + y1_in[t, 0]
        paired[t, y_down, 1] = paired[t, y_down, 1] + y1_in[t, 1]
        for copy in y2_copies(t):
            copy.start()

    def project(t):
        slot = lax.rem(t, 2)
        arrived(y2_in.at[t], y2_r.at[t])
        for c in range(2):
            for f in range(8):
                lanes = pl.ds(f * 128, 128)
                value = paired[t, y, c, :, lanes] + (y2_in[t, 0, c, :, lanes] + y2_in[t, 1, c, :, lanes])
                fold[pl.ds(c * 8 + f, 16, stride=16), :] = value

        leg_copy(t).wait()
        lane = lax.broadcasted_iota(jnp.int32, (16, 128), 1)
        even, low_half = lax.rem(lane, 2) == 0, lane < 64
        for owner in range(LAT_DEV):
            ox, oz = owner // 4, owner % 4
            rows = fold[owner * 16 : owner * 16 + 16, :]
            zero = jnp.zeros_like(rows)
            left = jnp.concatenate([jnp.where(even, rows, zero), jnp.where(even, zero, rows)], 0).astype(jnp.bfloat16)
            n = UNITS[ox]
            right = leg[slot, owner, :, :, 0 : 128 * n].reshape(128, 128 * n)
            value = jnp.dot(left, right, preferred_element_type=jnp.float32)
            for unit in range(n - 1):
                spec_z[t, oz, Z_OFFSETS[ox] + unit] = value[:, unit * 128 : unit * 128 + 128]
            last, first = value[:, (n - 1) * 128 : n * 128], X_OFFSETS[oz]
            if X_ROWS[oz] == 32:
                spec_x[t, ox, first : first + 32, :] = last
            else:
                spec_x[t, ox, first : first + 16, :] = jnp.where(low_half, last[0:16], pltpu.roll(last[16:32], 64, 1))
        for copy in (*z1_copies(t), *x1_copies(t)):
            copy.start()

        @pl.when(t + 2 < STEPS)
        def _():
            leg_copy(t + 2).start()

    def forward(t):
        arrived(z1_in.at[t], z1_r.at[t])
        spec_z[t, z_up, 0:z_half] = spec_z[t, z_up, 0:z_half] + z1_in[t, 0]
        spec_z[t, z_down, z_half:Z_TOTAL] = spec_z[t, z_down, z_half:Z_TOTAL] + z1_in[t, 1]
        for copy in z2_copies(t):
            copy.start()
        arrived(x1_in.at[t], x1_r.at[t])
        spec_x[t, x_up, 0:X_HALF] = spec_x[t, x_up, 0:X_HALF] + x1_in[t, 0]
        spec_x[t, x_down, X_HALF:X_TOTAL] = spec_x[t, x_down, X_HALF:X_TOTAL] + x1_in[t, 1]
        for copy in x2_copies(t):
            copy.start()

    def cross(t):
        arrived(z2_in.at[t], z2_r.at[t])
        spec_z[t, z] = spec_z[t, z] + (z2_in[t, 0] + z2_in[t, 1])
        for to in range(3):

            @pl.when(x != to)
            def _():
                zx_copy(t, x, to).start()

        arrived(x2_in.at[t], x2_r.at[t])
        spec_x[t, x] = spec_x[t, x] + (x2_in[t, 0] + x2_in[t, 1])
        for to in range(4):

            @pl.when(z != to)
            def _():
                xz_copy(t, z, to).start()

    def finish(t):
        i, level = lax.rem(t, CHUNKS), t // CHUNKS
        order = r + LON_DEV * (CHUNKS * k + i)
        lane = lax.broadcasted_iota(jnp.int32, (16, 128), 1)
        def write(unit, e, value):
            inside = order + 2 * (lane + unit * 128) + e < WAVES
            first = e * 512 + unit * 128
            first = first if isinstance(first, int) else pl.multiple_of(first, 128)
            result[i, level, :, pl.ds(first, 128)] = jnp.where(inside, value, jnp.zeros_like(value))

        for mine in range(4):

            @pl.when(x == mine)
            def _():
                n, first = Z_UNITS[mine], Z_OFFSETS[mine]
                others = [source for source in range(4) if source != mine]
                if n:
                    arrived(zx_in.at[t, 0:3, 0:n], zx_r.at[t])
                for e in range(2):
                    rows = pl.ds(e * 16, 16)
                    for unit in range(n):
                        value = spec_z[t, z, first + unit, rows, :]
                        for source in others:
                            value = value + zx_in[t, source, unit, rows, :]
                        write(unit, e, value)
                    for unit in range(n + 1, 4):
                        result[i, level, :, pl.ds(e * 512 + unit * 128, 128)] = jnp.zeros((16, 128), jnp.float32)

        for mine in range(4):

            @pl.when(z == mine)
            def _():
                n, first = X_ROWS[mine], X_OFFSETS[mine]
                others = [source for source in range(4) if source != mine]
                arrived(xz_in.at[t, 0:3, 0:n], xz_r.at[t])
                value = spec_x[t, x, first : first + n, :]
                for source in others:
                    value = value + xz_in[t, source, 0:n, :]
                write(3 - x, 0, value[0:16])
                write(3 - x, 1, value[16:32] if n == 32 else pltpu.roll(value, 64, 1))

        out_copy(t).start()

    def stage(run, t):
        @pl.when((t >= 0) & (t < STEPS))
        def _():
            run(t)

    def steps(step, carry):
        t = step - 4
        stage(y_forward, t)
        stage(project, t - 1)
        stage(forward, t - 2)
        stage(cross, t - 3)
        stage(pair_sum, t + 2)
        stage(finish, t - 4)
        stage(analyse, t + 4)

        @pl.when(t == 0)
        def _():
            fields(1)

        return carry

    lax.fori_loop(0, STEPS + 8, steps, 0)

    for t in range(STEPS - 2, STEPS):
        core_copy(t).wait_send()
    pairs = ((y1_in, y1_s), (y2_in, y2_s), (z1_in, z1_s), (z2_in, z2_s), (x1_in, x1_s), (x2_in, x2_s))
    for buffer, sems in pairs:
        for way in range(2):
            arrived(buffer.at[:, way], sems.at[way])
    for to in range(3):

        @pl.when(x != to)
        def _():
            arrived(zx_in.at[:, 0, 0 : Z_UNITS[to]], zx_s.at[to])

    for to in range(4):

        @pl.when(z != to)
        def _():
            arrived(xz_in.at[:, 0, 0 : X_ROWS[to]], xz_s.at[to])

    arrived(result, out_sem)


def local(grid, legendre):
    table = jnp.asarray(phase_table())
    f32, bf16 = jnp.float32, jnp.bfloat16
    dma = pltpu.SemaphoreType.DMA
    result = pl.pallas_call(
        kernel,
        out_shape=jax.ShapeDtypeStruct((CHUNKS, LEVELS, 16, WAVES), f32),
        in_specs=[pl.BlockSpec(memory_space=pl.ANY)] * 3,
        out_specs=pl.BlockSpec(memory_space=pl.ANY),
        scratch_shapes=[
            pltpu.VMEM((LEVELS, 12, 2, 64, LON_LOCAL), bf16),
            pltpu.VMEM((LEVELS, ROWS, LON_LOCAL), bf16),
            pltpu.VMEM((LEVELS, ROWS, LON_LOCAL), bf16),
            pltpu.VMEM((32, 32, 128), f32),
            pltpu.VMEM((CHUNKS, 8, 2, 16, LON_LOCAL), f32),
            pltpu.VMEM((512, LON_LOCAL), bf16),
            pltpu.VMEM((2, 2, 4, 2, 16, ROWS), f32),
            pltpu.VMEM((STEPS, 4, 2, 16, ROWS), f32),
            pltpu.VMEM((STEPS, 2, 16, ROWS), f32),
            pltpu.VMEM((STEPS, 2, 2, 16, ROWS), f32),
            pltpu.VMEM((256, 128), f32),
            pltpu.VMEM((2, 16, 64, 2, 512), bf16),
            pltpu.VMEM((STEPS, 4, Z_TOTAL, 32, 128), f32),
            pltpu.VMEM((STEPS, 4, X_TOTAL, 128), f32),
            pltpu.VMEM((STEPS, 2, Z_TOTAL // 2, 32, 128), f32),
            pltpu.VMEM((STEPS, 2, Z_TOTAL, 32, 128), f32),
            pltpu.VMEM((STEPS, 4, 3, 32, 128), f32),
            pltpu.VMEM((STEPS, 2, X_HALF, 128), f32),
            pltpu.VMEM((STEPS, 2, X_TOTAL, 128), f32),
            pltpu.VMEM((STEPS, 4, 32, 128), f32),
            pltpu.VMEM((CHUNKS, LEVELS, 16, WAVES), f32),
            dma((LEVELS,)),
            dma,
            dma((CHUNKS,)),
            dma((2,)),
            dma((STEPS,)),
            dma((STEPS,)),
            *[dma((count,)) for _ in range(6) for count in (2, STEPS)],
            *[dma((count,)) for _ in range(2) for count in (4, STEPS)],
        ],
        compiler_params=pltpu.CompilerParams(
            collective_id=0, has_side_effects=True, vmem_limit_bytes=62 * 2**20
        ),
        name="spectral",
    )(grid, table, legendre.reshape(LAT_DEV, CHUNKS, 64, 2, 512))
    spectral = result.reshape(1, CHUNKS, LEVELS, 2, 8, 2, WAVES // 2)
    return jnp.transpose(spectral, (0, 1, 4, 2, 3, 5, 6))


def solution(mesh):
    in_specs = (P(None, None, None, "lat", "lon"), P("lon", None, "lat", None, None))
    out_specs = P("lon", "lat", None, None, None, None, None)
    return jax.shard_map(local, mesh=mesh, in_specs=in_specs, out_specs=out_specs, check_vma=False)
```

```python
import jax
import jax.numpy as jnp
import numpy as np
from jax import lax
from jax.experimental import pallas as pl
from jax.experimental.pallas import tpu as pltpu
from jax.sharding import PartitionSpec as P

NLON = 4096
WAVES = 1024
LON_DEV = 8
LAT_DEV = 16
LON_LOCAL = NLON // LON_DEV
ROWS = 1024
CHUNKS = 8
LEVELS = 2
STEPS = CHUNKS * LEVELS
UNITS = (4, 3, 2, 1)
Z_UNITS = (3, 2, 1, 0)
Z_OFFSETS = (0, 3, 5, 6)
Z_TOTAL = 6
X_ROWS = (32, 32, 16, 16)
X_OFFSETS = (0, 32, 64, 80)
X_TOTAL = 96
X_HALF = X_TOTAL // 2
ADIABATIC = 0.286
ROOT_HALF = 0.5**0.5


def phase_table():
    i, core, y, k = np.meshgrid(
        np.arange(CHUNKS), np.arange(2), np.arange(4), np.arange(LAT_DEV), indexing="ij"
    )
    m = 2 * y + core + LON_DEV * (CHUNKS * k + i)
    turns = m[..., None] * np.arange(LON_LOCAL) % NLON
    angles = turns * (2.0 * np.pi / NLON)
    table = np.stack([np.cos(angles), -np.sin(angles)], 3) / np.sqrt(NLON)
    return table.reshape(CHUNKS, 8, 2, LAT_DEV, LON_LOCAL).astype(np.float32)


def eighth_cos(n):
    n = lax.rem(n, 8)
    value = jnp.float32(1.0)
    for at, root in ((1, ROOT_HALF), (2, 0.0), (3, -ROOT_HALF), (4, -1.0), (5, -ROOT_HALF), (6, 0.0), (7, ROOT_HALF)):
        value = jnp.where(n == at, jnp.float32(root), value)
    return value


def tendencies(f):
    u, v, zeta, div, temp, hum, temp_x, temp_y, hum_x, hum_y, press_x, press_y = f
    return (
        zeta * v - temp * press_x,
        -zeta * u - temp * press_y,
        u * v,
        -(u * temp_x + v * temp_y) + ADIABATIC * temp * div,
        -(u * hum_x + v * hum_y) - hum * div,
        u * temp,
        v * temp,
        v * hum,
    )


def split_bf16(a):
    high = a.astype(jnp.bfloat16)
    return high, (a - high.astype(jnp.float32)).astype(jnp.bfloat16)


NT = (((1,), (1,)), ((), ()))


def kernel(
    grid_ref, table_ref, leg_ref, out_ref,
    grid, t_hi, t_lo, mix, table, phases, part, paired, y1_in, y2_in, fold, leg,
    spec_z, spec_x, z1_in, z2_in, zx_in, x1_in, x2_in, xz_in, result,
    grid_sem, out_sem, table_sem, leg_sem, core_s, core_r, y1_s, y1_r, y2_s, y2_r,
    z1_s, z1_r, z2_s, z2_r, x1_s, x1_r, x2_s, x2_r, zx_s, zx_r, xz_s, xz_r,
):
    r = lax.axis_index("lon")
    k = lax.axis_index("lat")
    y, core = r // 2, lax.rem(r, 2)
    x, z = k // 4, lax.rem(k, 4)
    y_up, y_down = lax.rem(y + 1, 4), lax.rem(y + 3, 4)
    z_up, z_down = lax.rem(z + 1, 4), lax.rem(z + 3, 4)
    x_up, x_down = lax.rem(x + 1, 4), lax.rem(x + 3, 4)
    x_far, y_far, z_far = lax.rem(x + 2, 4), lax.rem(y + 2, 4), lax.rem(z + 2, 4)

    def lon_dev(yy, cc):
        return {"lon": yy * 2 + cc}

    def lat_dev(xx, zz):
        return {"lat": xx * 4 + zz}

    def send(src, dst, s, q, dev):
        return pltpu.make_async_remote_copy(
            src_ref=src, dst_ref=dst, send_sem=s, recv_sem=q, device_id=dev, device_id_type=pl.DeviceIdType.MESH
        )

    def arrived(ref, sem):
        pltpu.make_async_copy(ref, ref, sem).wait()

    def table_copy(t):
        return pltpu.make_async_copy(table_ref.at[t], table.at[t], table_sem.at[t])

    def leg_copy(t):
        slot = lax.rem(t, 2)
        return pltpu.make_async_copy(leg_ref.at[:, lax.rem(t, CHUNKS)], leg.at[slot], leg_sem.at[slot])

    def out_copy(t):
        at = (lax.rem(t, CHUNKS), t // CHUNKS)
        return pltpu.make_async_copy(result.at[at], out_ref.at[at], out_sem)

    def grid_copy(level):
        return pltpu.make_async_copy(grid_ref.at[:, level], grid.at[level], grid_sem.at[level])

    def core_copy(t):
        return send(
            part.at[lax.rem(t, 2), 1 - core], paired.at[t], core_s.at[t], core_r.at[t], lon_dev(y, 1 - core)
        )

    def y1_copies(t):
        return (
            send(paired.at[t, y_far, 0], y1_in.at[t, 0], y1_s.at[0], y1_r.at[t], lon_dev(y_up, core)),
            send(paired.at[t, y_far, 1], y1_in.at[t, 1], y1_s.at[1], y1_r.at[t], lon_dev(y_down, core)),
        )

    def y2_copies(t):
        return (
            send(paired.at[t, y_up], y2_in.at[t, 0], y2_s.at[0], y2_r.at[t], lon_dev(y_up, core)),
            send(paired.at[t, y_down], y2_in.at[t, 1], y2_s.at[1], y2_r.at[t], lon_dev(y_down, core)),
        )

    z_half = Z_TOTAL // 2

    def z1_copies(t):
        return (
            send(spec_z.at[t, z_far, 0:z_half], z1_in.at[t, 0], z1_s.at[0], z1_r.at[t], lat_dev(x, z_up)),
            send(spec_z.at[t, z_far, z_half:Z_TOTAL], z1_in.at[t, 1], z1_s.at[1], z1_r.at[t], lat_dev(x, z_down)),
        )

    def z2_copies(t):
        return (
            send(spec_z.at[t, z_up], z2_in.at[t, 0], z2_s.at[0], z2_r.at[t], lat_dev(x, z_up)),
            send(spec_z.at[t, z_down], z2_in.at[t, 1], z2_s.at[1], z2_r.at[t], lat_dev(x, z_down)),
        )

    def x1_copies(t):
        return (
            send(spec_x.at[t, x_far, 0:X_HALF], x1_in.at[t, 0], x1_s.at[0], x1_r.at[t], lat_dev(x_up, z)),
            send(spec_x.at[t, x_far, X_HALF:X_TOTAL], x1_in.at[t, 1], x1_s.at[1], x1_r.at[t], lat_dev(x_down, z)),
        )

    def x2_copies(t):
        return (
            send(spec_x.at[t, x_up], x2_in.at[t, 0], x2_s.at[0], x2_r.at[t], lat_dev(x_up, z)),
            send(spec_x.at[t, x_down], x2_in.at[t, 1], x2_s.at[1], x2_r.at[t], lat_dev(x_down, z)),
        )

    def zx_copy(t, source, to):
        n, first = Z_UNITS[to], Z_OFFSETS[to]
        return send(
            spec_z.at[t, z, first : first + n], zx_in.at[t, source, 0:n], zx_s.at[to], zx_r.at[t], lat_dev(to, z)
        )

    def xz_copy(t, source, to):
        n, first = X_ROWS[to], X_OFFSETS[to]
        return send(
            spec_x.at[t, x, first : first + n], xz_in.at[t, source, 0:n], xz_s.at[to], xz_r.at[t], lat_dev(x, to)
        )

    table_copy(0).start()
    grid_copy(0).start()
    grid_copy(1).start()
    for i in range(2):
        leg_copy(i).start()
    for i in range(1, CHUNKS):
        table_copy(i).start()

    barrier = pltpu.get_barrier_semaphore()
    neighbours = [lon_dev(y, 1 - core), lon_dev(y_up, core), lon_dev(y_down, core)]
    neighbours += [lat_dev(x, to) for to in (z_up, z_far, z_down)] + [lat_dev(to, z) for to in (x_up, x_far, x_down)]
    for dev in neighbours:
        pl.semaphore_signal(barrier, inc=1, device_id=dev, device_id_type=pl.DeviceIdType.MESH)

    def fields(level):
        grid_copy(level).wait()

        def rows16(block, carry):
            first = pl.multiple_of(block * 16, 16)
            for lane in range(4):
                lanes = pl.ds(lane * 128, 128)
                north, south = (
                    tendencies([grid[level, f, h, pl.ds(first, 16), lanes].astype(jnp.float32) for f in range(12)])
                    for h in range(2)
                )
                for t in range(8):
                    mix[lane * 8 + t, pl.ds(0, 16, stride=2), :] = north[t] + south[t]
                    mix[lane * 8 + t, pl.ds(1, 16, stride=2), :] = north[t] - south[t]
                for t in range(8):
                    high, low = split_bf16(mix[lane * 8 + t])
                    at = pl.multiple_of(t * 128 + block * 32, 32)
                    t_hi[level, pl.ds(at, 32), lanes] = high
                    t_lo[level, pl.ds(at, 32), lanes] = low
            return carry

        lax.fori_loop(0, 4, rows16, 0)

    def rotate(i):
        table_copy(i).wait()

        def block_of(block, carry):
            q = 2 * lax.rem(block, 4) + block // 4
            c, s = eighth_cos(r * q), eighth_cos(r * q + 6)
            real, imag = table[i, block, 0], table[i, block, 1]
            for part_index, value in enumerate((real * c + imag * s, imag * c - real * s)):
                high, low = split_bf16(value)
                at = pl.multiple_of(block * 32 + part_index * 16, 16)
                phases[i, pl.ds(at, 16), :] = high
                phases[i, pl.ds(at + 256, 16), :] = low
            return carry

        lax.fori_loop(0, 8, block_of, 0)

    rotate(0)
    fields(0)

    pl.semaphore_wait(barrier, len(neighbours))

    def analyse(t):
        slot, i, level = lax.rem(t, 2), lax.rem(t, CHUNKS), t // CHUNKS

        @pl.when(t >= 2)
        def _():
            core_copy(t - 2).wait_send()

        for n in range(ROWS // 256):
            rows = pl.ds(n * 256, 256)
            both = lax.dot_general(phases[i], t_hi[level, rows, :], NT, preferred_element_type=jnp.float32)
            rest = lax.dot_general(phases[i, 0:256, :], t_lo[level, rows, :], NT, preferred_element_type=jnp.float32)
            value = both[0:256] + (both[256:512] + rest)
            part[slot, :, :, :, :, rows] = value.reshape(2, 4, 2, 16, 256)
        core_copy(t).start()

        @pl.when(t + 1 < CHUNKS)
        def _():
            rotate(t + 1)

    def pair_sum(t):
        slot = lax.rem(t, 2)
        core_copy(t).wait_recv()

        def add(n, carry):
            yy = lax.rem(y_far + n, 4)
            paired[t, yy] = paired[t, yy] + part[slot, core, yy]
            return carry

        lax.fori_loop(0, 4, add, 0)
        for copy in y1_copies(t):
            copy.start()

    def y_forward(t):
        arrived(y1_in.at[t], y1_r.at[t])
        paired[t, y_up, 0] = paired[t, y_up, 0] + y1_in[t, 0]
        paired[t, y_down, 1] = paired[t, y_down, 1] + y1_in[t, 1]
        for copy in y2_copies(t):
            copy.start()

    def project(t):
        slot = lax.rem(t, 2)
        arrived(y2_in.at[t], y2_r.at[t])
        for c in range(2):
            for f in range(8):
                lanes = pl.ds(f * 128, 128)
                value = paired[t, y, c, :, lanes] + (y2_in[t, 0, c, :, lanes] + y2_in[t, 1, c, :, lanes])
                fold[pl.ds(c * 8 + f, 16, stride=16), :] = value

        leg_copy(t).wait()
        lane = lax.broadcasted_iota(jnp.int32, (16, 128), 1)
        even, low_half = lax.rem(lane, 2) == 0, lane < 64
        for owner in range(LAT_DEV):
            ox, oz = owner // 4, owner % 4
            rows = fold[owner * 16 : owner * 16 + 16, :]
            zero = jnp.zeros_like(rows)
            left = jnp.concatenate([jnp.where(even, rows, zero), jnp.where(even, zero, rows)], 0).astype(jnp.bfloat16)
            n = UNITS[ox]
            right = leg[slot, owner, :, :, 0 : 128 * n].reshape(128, 128 * n)
            value = jnp.dot(left, right, preferred_element_type=jnp.float32)
            for unit in range(n - 1):
                spec_z[t, oz, Z_OFFSETS[ox] + unit] = value[:, unit * 128 : unit * 128 + 128]
            last, first = value[:, (n - 1) * 128 : n * 128], X_OFFSETS[oz]
            if X_ROWS[oz] == 32:
                spec_x[t, ox, first : first + 32, :] = last
            else:
                spec_x[t, ox, first : first + 16, :] = jnp.where(low_half, last[0:16], pltpu.roll(last[16:32], 64, 1))
        for copy in (*z1_copies(t), *x1_copies(t)):
            copy.start()

        @pl.when(t + 2 < STEPS)
        def _():
            leg_copy(t + 2).start()

    def forward(t):
        arrived(z1_in.at[t], z1_r.at[t])
        spec_z[t, z_up, 0:z_half] = spec_z[t, z_up, 0:z_half] + z1_in[t, 0]
        spec_z[t, z_down, z_half:Z_TOTAL] = spec_z[t, z_down, z_half:Z_TOTAL] + z1_in[t, 1]
        for copy in z2_copies(t):
            copy.start()
        arrived(x1_in.at[t], x1_r.at[t])
        spec_x[t, x_up, 0:X_HALF] = spec_x[t, x_up, 0:X_HALF] + x1_in[t, 0]
        spec_x[t, x_down, X_HALF:X_TOTAL] = spec_x[t, x_down, X_HALF:X_TOTAL] + x1_in[t, 1]
        for copy in x2_copies(t):
            copy.start()

    def cross(t):
        arrived(z2_in.at[t], z2_r.at[t])
        spec_z[t, z] = spec_z[t, z] + (z2_in[t, 0] + z2_in[t, 1])
        for to in range(3):

            @pl.when(x != to)
            def _():
                zx_copy(t, x, to).start()

        arrived(x2_in.at[t], x2_r.at[t])
        spec_x[t, x] = spec_x[t, x] + (x2_in[t, 0] + x2_in[t, 1])
        for to in range(4):

            @pl.when(z != to)
            def _():
                xz_copy(t, z, to).start()

    def finish(t):
        i, level = lax.rem(t, CHUNKS), t // CHUNKS
        order = r + LON_DEV * (CHUNKS * k + i)
        lane = lax.broadcasted_iota(jnp.int32, (16, 128), 1)
        def write(unit, e, value):
            inside = order + 2 * (lane + unit * 128) + e < WAVES
            first = e * 512 + unit * 128
            first = first if isinstance(first, int) else pl.multiple_of(first, 128)
            result[i, level, :, pl.ds(first, 128)] = jnp.where(inside, value, jnp.zeros_like(value))

        for mine in range(4):

            @pl.when(x == mine)
            def _():
                n, first = Z_UNITS[mine], Z_OFFSETS[mine]
                others = [source for source in range(4) if source != mine]
                if n:
                    arrived(zx_in.at[t, 0:3, 0:n], zx_r.at[t])
                for e in range(2):
                    rows = pl.ds(e * 16, 16)
                    for unit in range(n):
                        value = spec_z[t, z, first + unit, rows, :]
                        for source in others:
                            value = value + zx_in[t, source, unit, rows, :]
                        write(unit, e, value)
                    for unit in range(n + 1, 4):
                        result[i, level, :, pl.ds(e * 512 + unit * 128, 128)] = jnp.zeros((16, 128), jnp.float32)

        for mine in range(4):

            @pl.when(z == mine)
            def _():
                n, first = X_ROWS[mine], X_OFFSETS[mine]
                others = [source for source in range(4) if source != mine]
                arrived(xz_in.at[t, 0:3, 0:n], xz_r.at[t])
                value = spec_x[t, x, first : first + n, :]
                for source in others:
                    value = value + xz_in[t, source, 0:n, :]
                write(3 - x, 0, value[0:16])
                write(3 - x, 1, value[16:32] if n == 32 else pltpu.roll(value, 64, 1))

        out_copy(t).start()

    def stage(run, t):
        @pl.when((t >= 0) & (t < STEPS))
        def _():
            run(t)

    def steps(step, carry):
        t = step - 4
        stage(y_forward, t)
        stage(project, t - 1)
        stage(pair_sum, t + 2)
        stage(forward, t - 2)
        stage(cross, t - 3)
        stage(finish, t - 4)
        stage(analyse, t + 4)

        @pl.when(t == 0)
        def _():
            fields(1)

        return carry

    lax.fori_loop(0, STEPS + 8, steps, 0)

    for t in range(STEPS - 2, STEPS):
        core_copy(t).wait_send()
    pairs = ((y1_in, y1_s), (y2_in, y2_s), (z1_in, z1_s), (z2_in, z2_s), (x1_in, x1_s), (x2_in, x2_s))
    for buffer, sems in pairs:
        for way in range(2):
            arrived(buffer.at[:, way], sems.at[way])
    for to in range(3):

        @pl.when(x != to)
        def _():
            arrived(zx_in.at[:, 0, 0 : Z_UNITS[to]], zx_s.at[to])

    for to in range(4):

        @pl.when(z != to)
        def _():
            arrived(xz_in.at[:, 0, 0 : X_ROWS[to]], xz_s.at[to])

    arrived(result, out_sem)


def local(grid, legendre):
    table = jnp.asarray(phase_table())
    f32, bf16 = jnp.float32, jnp.bfloat16
    dma = pltpu.SemaphoreType.DMA
    result = pl.pallas_call(
        kernel,
        out_shape=jax.ShapeDtypeStruct((CHUNKS, LEVELS, 16, WAVES), f32),
        in_specs=[pl.BlockSpec(memory_space=pl.ANY)] * 3,
        out_specs=pl.BlockSpec(memory_space=pl.ANY),
        scratch_shapes=[
            pltpu.VMEM((LEVELS, 12, 2, 64, LON_LOCAL), bf16),
            pltpu.VMEM((LEVELS, ROWS, LON_LOCAL), bf16),
            pltpu.VMEM((LEVELS, ROWS, LON_LOCAL), bf16),
            pltpu.VMEM((32, 32, 128), f32),
            pltpu.VMEM((CHUNKS, 8, 2, 16, LON_LOCAL), f32),
            pltpu.VMEM((CHUNKS, 512, LON_LOCAL), bf16),
            pltpu.VMEM((2, 2, 4, 2, 16, ROWS), f32),
            pltpu.VMEM((STEPS, 4, 2, 16, ROWS), f32),
            pltpu.VMEM((STEPS, 2, 16, ROWS), f32),
            pltpu.VMEM((STEPS, 2, 2, 16, ROWS), f32),
            pltpu.VMEM((256, 128), f32),
            pltpu.VMEM((2, 16, 64, 2, 512), bf16),
            pltpu.VMEM((STEPS, 4, Z_TOTAL, 32, 128), f32),
            pltpu.VMEM((STEPS, 4, X_TOTAL, 128), f32),
            pltpu.VMEM((STEPS, 2, Z_TOTAL // 2, 32, 128), f32),
            pltpu.VMEM((STEPS, 2, Z_TOTAL, 32, 128), f32),
            pltpu.VMEM((STEPS, 4, 3, 32, 128), f32),
            pltpu.VMEM((STEPS, 2, X_HALF, 128), f32),
            pltpu.VMEM((STEPS, 2, X_TOTAL, 128), f32),
            pltpu.VMEM((STEPS, 4, 32, 128), f32),
            pltpu.VMEM((CHUNKS, LEVELS, 16, WAVES), f32),
            dma((LEVELS,)),
            dma,
            dma((CHUNKS,)),
            dma((2,)),
            dma((STEPS,)),
            dma((STEPS,)),
            *[dma((count,)) for _ in range(6) for count in (2, STEPS)],
            *[dma((count,)) for _ in range(2) for count in (4, STEPS)],
        ],
        compiler_params=pltpu.CompilerParams(
            collective_id=0, has_side_effects=True, vmem_limit_bytes=62 * 2**20
        ),
        name="spectral",
    )(grid, table, legendre.reshape(LAT_DEV, CHUNKS, 64, 2, 512))
    spectral = result.reshape(1, CHUNKS, LEVELS, 2, 8, 2, WAVES // 2)
    return jnp.transpose(spectral, (0, 1, 4, 2, 3, 5, 6))


def solution(mesh):
    in_specs = (P(None, None, None, "lat", "lon"), P("lon", None, "lat", None, None))
    out_specs = P("lon", "lat", None, None, None, None, None)
    return jax.shard_map(local, mesh=mesh, in_specs=in_specs, out_specs=out_specs, check_vma=False)
```

```python
import jax
import jax.numpy as jnp
import numpy as np
from jax import lax
from jax.experimental import pallas as pl
from jax.experimental.pallas import tpu as pltpu
from jax.sharding import PartitionSpec as P

NLON = 4096
WAVES = 1024
LON_DEV = 8
LAT_DEV = 16
LON_LOCAL = NLON // LON_DEV
ROWS = 1024
CHUNKS = 8
LEVELS = 2
STEPS = CHUNKS * LEVELS
UNITS = (4, 3, 2, 1)
Z_UNITS = (3, 2, 1, 0)
Z_OFFSETS = (0, 3, 5, 6)
Z_TOTAL = 6
X_ROWS = (32, 32, 16, 16)
X_OFFSETS = (0, 32, 64, 80)
X_TOTAL = 96
X_HALF = X_TOTAL // 2
ADIABATIC = 0.286
ROOT_HALF = 0.5**0.5


def phase_table():
    i, core, y, k = np.meshgrid(
        np.arange(CHUNKS), np.arange(2), np.arange(4), np.arange(LAT_DEV), indexing="ij"
    )
    m = 2 * y + core + LON_DEV * (CHUNKS * k + i)
    turns = m[..., None] * np.arange(LON_LOCAL) % NLON
    angles = turns * (2.0 * np.pi / NLON)
    table = np.stack([np.cos(angles), -np.sin(angles)], 3) / np.sqrt(NLON)
    return table.reshape(CHUNKS, 8, 2, LAT_DEV, LON_LOCAL).astype(np.float32)


def eighth_cos(n):
    n = lax.rem(n, 8)
    value = jnp.float32(1.0)
    for at, root in ((1, ROOT_HALF), (2, 0.0), (3, -ROOT_HALF), (4, -1.0), (5, -ROOT_HALF), (6, 0.0), (7, ROOT_HALF)):
        value = jnp.where(n == at, jnp.float32(root), value)
    return value


def tendencies(f):
    u, v, zeta, div, temp, hum, temp_x, temp_y, hum_x, hum_y, press_x, press_y = f
    return (
        zeta * v - temp * press_x,
        -zeta * u - temp * press_y,
        u * v,
        -(u * temp_x + v * temp_y) + ADIABATIC * temp * div,
        -(u * hum_x + v * hum_y) - hum * div,
        u * temp,
        v * temp,
        v * hum,
    )


def split_bf16(a):
    high = a.astype(jnp.bfloat16)
    return high, (a - high.astype(jnp.float32)).astype(jnp.bfloat16)


NT = (((1,), (1,)), ((), ()))


def kernel(
    grid_ref, table_ref, leg_ref, out_ref,
    grid, t_hi, t_lo, mix, table, phases, part, paired, y1_in, y2_in, fold, leg,
    spec_z, spec_x, z1_in, z2_in, zx_in, x1_in, x2_in, xz_in, result,
    grid_sem, out_sem, table_sem, leg_sem, core_s, core_r, y1_s, y1_r, y2_s, y2_r,
    z1_s, z1_r, z2_s, z2_r, x1_s, x1_r, x2_s, x2_r, zx_s, zx_r, xz_s, xz_r,
):
    r = lax.axis_index("lon")
    k = lax.axis_index("lat")
    y, core = r // 2, lax.rem(r, 2)
    x, z = k // 4, lax.rem(k, 4)
    y_up, y_down = lax.rem(y + 1, 4), lax.rem(y + 3, 4)
    z_up, z_down = lax.rem(z + 1, 4), lax.rem(z + 3, 4)
    x_up, x_down = lax.rem(x + 1, 4), lax.rem(x + 3, 4)
    x_far, y_far, z_far = lax.rem(x + 2, 4), lax.rem(y + 2, 4), lax.rem(z + 2, 4)

    def lon_dev(yy, cc):
        return {"lon": yy * 2 + cc}

    def lat_dev(xx, zz):
        return {"lat": xx * 4 + zz}

    def send(src, dst, s, q, dev):
        return pltpu.make_async_remote_copy(
            src_ref=src, dst_ref=dst, send_sem=s, recv_sem=q, device_id=dev, device_id_type=pl.DeviceIdType.MESH
        )

    def arrived(ref, sem):
        pltpu.make_async_copy(ref, ref, sem).wait()

    def table_copy(t):
        return pltpu.make_async_copy(table_ref.at[t], table.at[t], table_sem.at[t])

    def leg_copy(t):
        slot = lax.rem(t, 2)
        return pltpu.make_async_copy(leg_ref.at[:, lax.rem(t, CHUNKS)], leg.at[slot], leg_sem.at[slot])

    def out_copy(t):
        at = (lax.rem(t, CHUNKS), t // CHUNKS)
        return pltpu.make_async_copy(result.at[at], out_ref.at[at], out_sem)

    def grid_copy(level):
        return pltpu.make_async_copy(grid_ref.at[:, level], grid.at[level], grid_sem.at[level])

    def core_copy(t):
        return send(
            part.at[lax.rem(t, 2), 1 - core], paired.at[t], core_s.at[t], core_r.at[t], lon_dev(y, 1 - core)
        )

    def y1_copies(t):
        return (
            send(paired.at[t, y_far, 0], y1_in.at[t, 0], y1_s.at[0], y1_r.at[t], lon_dev(y_up, core)),
            send(paired.at[t, y_far, 1], y1_in.at[t, 1], y1_s.at[1], y1_r.at[t], lon_dev(y_down, core)),
        )

    def y2_copies(t):
        return (
            send(paired.at[t, y_up], y2_in.at[t, 0], y2_s.at[0], y2_r.at[t], lon_dev(y_up, core)),
            send(paired.at[t, y_down], y2_in.at[t, 1], y2_s.at[1], y2_r.at[t], lon_dev(y_down, core)),
        )

    z_half = Z_TOTAL // 2

    def z1_copies(t):
        return (
            send(spec_z.at[t, z_far, 0:z_half], z1_in.at[t, 0], z1_s.at[0], z1_r.at[t], lat_dev(x, z_up)),
            send(spec_z.at[t, z_far, z_half:Z_TOTAL], z1_in.at[t, 1], z1_s.at[1], z1_r.at[t], lat_dev(x, z_down)),
        )

    def z2_copies(t):
        return (
            send(spec_z.at[t, z_up], z2_in.at[t, 0], z2_s.at[0], z2_r.at[t], lat_dev(x, z_up)),
            send(spec_z.at[t, z_down], z2_in.at[t, 1], z2_s.at[1], z2_r.at[t], lat_dev(x, z_down)),
        )

    def x1_copies(t):
        return (
            send(spec_x.at[t, x_far, 0:X_HALF], x1_in.at[t, 0], x1_s.at[0], x1_r.at[t], lat_dev(x_up, z)),
            send(spec_x.at[t, x_far, X_HALF:X_TOTAL], x1_in.at[t, 1], x1_s.at[1], x1_r.at[t], lat_dev(x_down, z)),
        )

    def x2_copies(t):
        return (
            send(spec_x.at[t, x_up], x2_in.at[t, 0], x2_s.at[0], x2_r.at[t], lat_dev(x_up, z)),
            send(spec_x.at[t, x_down], x2_in.at[t, 1], x2_s.at[1], x2_r.at[t], lat_dev(x_down, z)),
        )

    def zx_copy(t, source, to):
        n, first = Z_UNITS[to], Z_OFFSETS[to]
        return send(
            spec_z.at[t, z, first : first + n], zx_in.at[t, source, 0:n], zx_s.at[to], zx_r.at[t], lat_dev(to, z)
        )

    def xz_copy(t, source, to):
        n, first = X_ROWS[to], X_OFFSETS[to]
        return send(
            spec_x.at[t, x, first : first + n], xz_in.at[t, source, 0:n], xz_s.at[to], xz_r.at[t], lat_dev(x, to)
        )

    table_copy(0).start()
    grid_copy(0).start()
    grid_copy(1).start()
    for i in range(2):
        leg_copy(i).start()
    for i in range(1, CHUNKS):
        table_copy(i).start()

    barrier = pltpu.get_barrier_semaphore()
    neighbours = [lon_dev(y, 1 - core), lon_dev(y_up, core), lon_dev(y_down, core)]
    neighbours += [lat_dev(x, to) for to in (z_up, z_far, z_down)] + [lat_dev(to, z) for to in (x_up, x_far, x_down)]
    for dev in neighbours:
        pl.semaphore_signal(barrier, inc=1, device_id=dev, device_id_type=pl.DeviceIdType.MESH)

    def fields(level):
        grid_copy(level).wait()

        def rows16(block, carry):
            first = pl.multiple_of(block * 16, 16)
            for lane in range(4):
                lanes = pl.ds(lane * 128, 128)
                north, south = (
                    tendencies([grid[level, f, h, pl.ds(first, 16), lanes].astype(jnp.float32) for f in range(12)])
                    for h in range(2)
                )
                for t in range(8):
                    mix[lane * 8 + t, pl.ds(0, 16, stride=2), :] = north[t] + south[t]
                    mix[lane * 8 + t, pl.ds(1, 16, stride=2), :] = north[t] - south[t]
                for t in range(8):
                    high, low = split_bf16(mix[lane * 8 + t])
                    at = pl.multiple_of(t * 128 + block * 32, 32)
                    t_hi[level, pl.ds(at, 32), lanes] = high
                    t_lo[level, pl.ds(at, 32), lanes] = low
            return carry

        lax.fori_loop(0, 4, rows16, 0)

    def rotate(i):
        table_copy(i).wait()

        def block_of(block, carry):
            q = 2 * lax.rem(block, 4) + block // 4
            c, s = eighth_cos(r * q), eighth_cos(r * q + 6)
            real, imag = table[i, block, 0], table[i, block, 1]
            for part_index, value in enumerate((real * c + imag * s, imag * c - real * s)):
                high, low = split_bf16(value)
                at = pl.multiple_of(block * 32 + part_index * 16, 16)
                phases[i, pl.ds(at, 16), :] = high
                phases[i, pl.ds(at + 256, 16), :] = low
            return carry

        lax.fori_loop(0, 8, block_of, 0)

    rotate(0)
    fields(0)

    pl.semaphore_wait(barrier, len(neighbours))

    def analyse(t):
        slot, i, level = lax.rem(t, 2), lax.rem(t, CHUNKS), t // CHUNKS

        @pl.when(t >= 2)
        def _():
            core_copy(t - 2).wait_send()

        for n in range(ROWS // 256):
            rows = pl.ds(n * 256, 256)
            both = lax.dot_general(phases[i], t_hi[level, rows, :], NT, preferred_element_type=jnp.float32)
            rest = lax.dot_general(phases[i, 0:256, :], t_lo[level, rows, :], NT, preferred_element_type=jnp.float32)
            value = both[0:256] + (both[256:512] + rest)
            part[slot, :, :, :, :, rows] = value.reshape(2, 4, 2, 16, 256)
        core_copy(t).start()

        @pl.when(t + 1 < CHUNKS)
        def _():
            rotate(t + 1)

    def pair_sum(t):
        slot = lax.rem(t, 2)
        core_copy(t).wait_recv()

        def add(n, carry):
            yy = lax.rem(y_far + n, 4)
            paired[t, yy] = paired[t, yy] + part[slot, core, yy]
            return carry

        lax.fori_loop(0, 4, add, 0)
        for copy in y1_copies(t):
            copy.start()

    def y_forward(t):
        arrived(y1_in.at[t], y1_r.at[t])
        paired[t, y_up, 0] = paired[t, y_up, 0] + y1_in[t, 0]
        paired[t, y_down, 1] = paired[t, y_down, 1] + y1_in[t, 1]
        for copy in y2_copies(t):
            copy.start()

    def project(t):
        slot = lax.rem(t, 2)
        arrived(y2_in.at[t], y2_r.at[t])
        for c in range(2):
            for f in range(8):
                lanes = pl.ds(f * 128, 128)
                value = paired[t, y, c, :, lanes] + (y2_in[t, 0, c, :, lanes] + y2_in[t, 1, c, :, lanes])
                fold[pl.ds(c * 8 + f, 16, stride=16), :] = value

        leg_copy(t).wait()
        lane = lax.broadcasted_iota(jnp.int32, (16, 128), 1)
        even, low_half = lax.rem(lane, 2) == 0, lane < 64
        for owner in range(LAT_DEV):
            ox, oz = owner // 4, owner % 4
            rows = fold[owner * 16 : owner * 16 + 16, :]
            zero = jnp.zeros_like(rows)
            left = jnp.concatenate([jnp.where(even, rows, zero), jnp.where(even, zero, rows)], 0).astype(jnp.bfloat16)
            n = UNITS[ox]
            right = leg[slot, owner, :, :, 0 : 128 * n].reshape(128, 128 * n)
            value = jnp.dot(left, right, preferred_element_type=jnp.float32)
            for unit in range(n - 1):
                spec_z[t, oz, Z_OFFSETS[ox] + unit] = value[:, unit * 128 : unit * 128 + 128]
            last, first = value[:, (n - 1) * 128 : n * 128], X_OFFSETS[oz]
            if X_ROWS[oz] == 32:
                spec_x[t, ox, first : first + 32, :] = last
            else:
                spec_x[t, ox, first : first + 16, :] = jnp.where(low_half, last[0:16], pltpu.roll(last[16:32], 64, 1))
        for copy in (*z1_copies(t), *x1_copies(t)):
            copy.start()

        @pl.when(t + 2 < STEPS)
        def _():
            leg_copy(t + 2).start()

    def forward(t):
        arrived(z1_in.at[t], z1_r.at[t])
        spec_z[t, z_up, 0:z_half] = spec_z[t, z_up, 0:z_half] + z1_in[t, 0]
        spec_z[t, z_down, z_half:Z_TOTAL] = spec_z[t, z_down, z_half:Z_TOTAL] + z1_in[t, 1]
        for copy in z2_copies(t):
            copy.start()
        arrived(x1_in.at[t], x1_r.at[t])
        spec_x[t, x_up, 0:X_HALF] = spec_x[t, x_up, 0:X_HALF] + x1_in[t, 0]
        spec_x[t, x_down, X_HALF:X_TOTAL] = spec_x[t, x_down, X_HALF:X_TOTAL] + x1_in[t, 1]
        for copy in x2_copies(t):
            copy.start()

    def cross(t):
        arrived(z2_in.at[t], z2_r.at[t])
        spec_z[t, z] = spec_z[t, z] + (z2_in[t, 0] + z2_in[t, 1])
        for to in range(3):

            @pl.when(x != to)
            def _():
                zx_copy(t, x, to).start()

        arrived(x2_in.at[t], x2_r.at[t])
        spec_x[t, x] = spec_x[t, x] + (x2_in[t, 0] + x2_in[t, 1])
        for to in range(4):

            @pl.when(z != to)
            def _():
                xz_copy(t, z, to).start()

    def finish(t):
        i, level = lax.rem(t, CHUNKS), t // CHUNKS
        order = r + LON_DEV * (CHUNKS * k + i)
        lane = lax.broadcasted_iota(jnp.int32, (16, 128), 1)
        def write(unit, e, value):
            inside = order + 2 * (lane + unit * 128) + e < WAVES
            first = e * 512 + unit * 128
            first = first if isinstance(first, int) else pl.multiple_of(first, 128)
            result[i, level, :, pl.ds(first, 128)] = jnp.where(inside, value, jnp.zeros_like(value))

        for mine in range(4):

            @pl.when(x == mine)
            def _():
                n, first = Z_UNITS[mine], Z_OFFSETS[mine]
                others = [source for source in range(4) if source != mine]
                if n:
                    arrived(zx_in.at[t, 0:3, 0:n], zx_r.at[t])
                for e in range(2):
                    rows = pl.ds(e * 16, 16)
                    for unit in range(n):
                        value = spec_z[t, z, first + unit, rows, :]
                        for source in others:
                            value = value + zx_in[t, source, unit, rows, :]
                        write(unit, e, value)
                    for unit in range(n + 1, 4):
                        result[i, level, :, pl.ds(e * 512 + unit * 128, 128)] = jnp.zeros((16, 128), jnp.float32)

        for mine in range(4):

            @pl.when(z == mine)
            def _():
                n, first = X_ROWS[mine], X_OFFSETS[mine]
                others = [source for source in range(4) if source != mine]
                arrived(xz_in.at[t, 0:3, 0:n], xz_r.at[t])
                value = spec_x[t, x, first : first + n, :]
                for source in others:
                    value = value + xz_in[t, source, 0:n, :]
                write(3 - x, 0, value[0:16])
                write(3 - x, 1, value[16:32] if n == 32 else pltpu.roll(value, 64, 1))

        out_copy(t).start()

    def stage(run, t):
        @pl.when((t >= 0) & (t < STEPS))
        def _():
            run(t)

    def steps(step, carry):
        t = step - 4
        stage(y_forward, t)
        stage(project, t - 1)
        stage(pair_sum, t + 2)
        stage(forward, t - 2)
        stage(cross, t - 3)
        stage(finish, t - 4)
        stage(analyse, t + 4)

        @pl.when(t == 3)
        def _():
            fields(1)

        return carry

    lax.fori_loop(0, STEPS + 8, steps, 0)

    for t in range(STEPS - 2, STEPS):
        core_copy(t).wait_send()
    pairs = ((y1_in, y1_s), (y2_in, y2_s), (z1_in, z1_s), (z2_in, z2_s), (x1_in, x1_s), (x2_in, x2_s))
    for buffer, sems in pairs:
        for way in range(2):
            arrived(buffer.at[:, way], sems.at[way])
    for to in range(3):

        @pl.when(x != to)
        def _():
            arrived(zx_in.at[:, 0, 0 : Z_UNITS[to]], zx_s.at[to])

    for to in range(4):

        @pl.when(z != to)
        def _():
            arrived(xz_in.at[:, 0, 0 : X_ROWS[to]], xz_s.at[to])

    arrived(result, out_sem)


def local(grid, legendre):
    table = jnp.asarray(phase_table())
    f32, bf16 = jnp.float32, jnp.bfloat16
    dma = pltpu.SemaphoreType.DMA
    result = pl.pallas_call(
        kernel,
        out_shape=jax.ShapeDtypeStruct((CHUNKS, LEVELS, 16, WAVES), f32),
        in_specs=[pl.BlockSpec(memory_space=pl.ANY)] * 3,
        out_specs=pl.BlockSpec(memory_space=pl.ANY),
        scratch_shapes=[
            pltpu.VMEM((LEVELS, 12, 2, 64, LON_LOCAL), bf16),
            pltpu.VMEM((LEVELS, ROWS, LON_LOCAL), bf16),
            pltpu.VMEM((LEVELS, ROWS, LON_LOCAL), bf16),
            pltpu.VMEM((32, 32, 128), f32),
            pltpu.VMEM((CHUNKS, 8, 2, 16, LON_LOCAL), f32),
            pltpu.VMEM((CHUNKS, 512, LON_LOCAL), bf16),
            pltpu.VMEM((2, 2, 4, 2, 16, ROWS), f32),
            pltpu.VMEM((STEPS, 4, 2, 16, ROWS), f32),
            pltpu.VMEM((STEPS, 2, 16, ROWS), f32),
            pltpu.VMEM((STEPS, 2, 2, 16, ROWS), f32),
            pltpu.VMEM((256, 128), f32),
            pltpu.VMEM((2, 16, 64, 2, 512), bf16),
            pltpu.VMEM((STEPS, 4, Z_TOTAL, 32, 128), f32),
            pltpu.VMEM((STEPS, 4, X_TOTAL, 128), f32),
            pltpu.VMEM((STEPS, 2, Z_TOTAL // 2, 32, 128), f32),
            pltpu.VMEM((STEPS, 2, Z_TOTAL, 32, 128), f32),
            pltpu.VMEM((STEPS, 4, 3, 32, 128), f32),
            pltpu.VMEM((STEPS, 2, X_HALF, 128), f32),
            pltpu.VMEM((STEPS, 2, X_TOTAL, 128), f32),
            pltpu.VMEM((STEPS, 4, 32, 128), f32),
            pltpu.VMEM((CHUNKS, LEVELS, 16, WAVES), f32),
            dma((LEVELS,)),
            dma,
            dma((CHUNKS,)),
            dma((2,)),
            dma((STEPS,)),
            dma((STEPS,)),
            *[dma((count,)) for _ in range(6) for count in (2, STEPS)],
            *[dma((count,)) for _ in range(2) for count in (4, STEPS)],
        ],
        compiler_params=pltpu.CompilerParams(
            collective_id=0, has_side_effects=True, vmem_limit_bytes=62 * 2**20
        ),
        name="spectral",
    )(grid, table, legendre.reshape(LAT_DEV, CHUNKS, 64, 2, 512))
    spectral = result.reshape(1, CHUNKS, LEVELS, 2, 8, 2, WAVES // 2)
    return jnp.transpose(spectral, (0, 1, 4, 2, 3, 5, 6))


def solution(mesh):
    in_specs = (P(None, None, None, "lat", "lon"), P("lon", None, "lat", None, None))
    out_specs = P("lon", "lat", None, None, None, None, None)
    return jax.shard_map(local, mesh=mesh, in_specs=in_specs, out_specs=out_specs, check_vma=False)
```
